512 devices in a mesh: dp: 32 (over y, x), expert: 16 (over z, core).
Axes of the slice: x: 4, y: 8, z: 8, core: 2. Of those that a mesh axis runs over, the one named last changes fastest.
Arguments:
- tokens: bfloat16 [65536, 1024], P(('dp', 'expert')), may hold values from -6 to 6
- cotangent: bfloat16 [65536, 1024], P(('dp', 'expert')), may hold values from -6 to 6
- routing: int32 [65536, 10], P(('dp', 'expert')), may hold values from 0 to 15, all different within a row; in each aligned block of 128 rows (0 to 127, 128 to 255, ...) at most 96 rows name the same one
- gates: bfloat16 [65536, 10], P(('dp', 'expert')), may hold values from 0.049804688 to 1
- gate_weight: bfloat16 [16, 1024, 256], P('expert'), may hold values from -0.1875 to 0.1875
- up_weight: bfloat16 [16, 1024, 256], P('expert'), may hold values from -0.1875 to 0.1875
- down_weight: bfloat16 [16, 256, 1024], P('expert'), may hold values from -0.375 to 0.375
Outputs:
- token_grad: bfloat16 [65536, 1024], P(('dp', 'expert'))
- gate_grad: bfloat16 [65536, 10], P(('dp', 'expert'))
- grad_gate: float32 [16, 1024, 256], P('expert', 'dp')
- grad_up: float32 [16, 1024, 256], P('expert', 'dp')
- grad_down: float32 [16, 256, 1024], P('expert', 'dp')
The draws below stay inside these ranges and needn't reach their ends.
Inputs may be any that keep to these rules, and one draw needn't show every extreme that they name: `routing`: each row names 10 different experts; among the rows of one device no expert is named by more than 96 rows, a bound that some block reaches.
All inputs are finite; a program needn't handle non-finite values.
Results may differ from the reference program's by a relative error of at most 0.02.
Values may be sent and summed in bfloat16 or wider, within the bound.
No kernel may reach another device: no remote copies, remote signals or barrier semaphores. Data moves between devices by JAX's collectives and lax.ppermute only.
A program may use at most 64 MiB of HBM per device.

```python
import math
import jax
import jax.numpy as jnp
import numpy as np
from jax import lax

D = 1024
F = 256
EXPERTS = 16
TOP = 10
TOK_DEV = 128
CAP = 96
TOKENS = 65536
N_DP = 32
N_EXPERT = 16


def steps_of(stream_key, shape, pieces, low, largest):
    def one(dim, shards_of):
        heights = jax.random.uniform(jax.random.fold_in(jax.random.fold_in(stream_key, 6), dim), (shards_of,), jnp.float32, low / len(pieces), largest / len(pieces))
        return jnp.repeat(jnp.exp(heights), shape[dim] // shards_of).reshape((-1,) + (1,) * (len(shape) - dim - 1))

    gain = one(*pieces[0])
    for cut in pieces[1:]:
        gain = gain * one(*cut)
    return gain


def assign_block(rng, own, number, rows, amount, top, bound, skew):
    sequence = jax.random.permutation(rng, amount)
    crowded, ordinary = portions_of(amount, rows * top, bound, skew, True), portions_of(amount, rows * top, bound, skew, False)
    places = jnp.arange(amount)

    def named(sizes, rotation):
        used = int((sizes > 0).sum())
        fixed = max(1, used // 4)
        passed = fixed + (places - fixed + rotation * (used - fixed)) % max(1, amount - fixed)
        return jnp.zeros((amount,), jnp.int32).at[sequence[jnp.where(places < fixed, places, passed)]].set(jnp.asarray(sizes, jnp.int32))

    sizes = jnp.where(number % 4 == 0, named(crowded, number // 4), named(ordinary, number - number // 4 - 1))
    mixed = jax.random.permutation(jax.random.fold_in(own, 3), amount)
    source_of, receiver = mixed[0:amount // 2 * 2:2], mixed[1:amount // 2 * 2:2]
    margin = jnp.minimum(sizes[source_of] - 1, bound - sizes[receiver]) // 2
    margin = jnp.where((source_of == sequence[0]) | (receiver == sequence[0]) | (sizes[receiver] == 0), 0, jnp.maximum(margin, 0))
    passed = jax.random.randint(jax.random.fold_in(own, 4), (amount // 2,), 0, 1 << 20) % (margin + 1)
    sizes = sizes.at[source_of].add(-passed).at[receiver].add(passed)
    labels = jnp.searchsorted(jnp.cumsum(sizes), jnp.arange(rows * top), side="right").astype(jnp.int32)
    table = labels.reshape(top, rows).T
    table = table[jax.random.permutation(jax.random.fold_in(own, 1), rows)]
    rotation = jax.random.randint(jax.random.fold_in(own, 2), (rows, 1), 0, top)
    return jnp.take_along_axis(table, (jnp.arange(top)[None, :] + rotation) % top, axis=1)


def portions_of(number_of, total, most, skew, full):
    loads = [(1 << 20) // math.isqrt(rank ** skew) + 1 for rank in range(1, number_of + 1)]
    largest = most if full else min(most, max(-(-total // number_of), total * loads[0] // sum(loads)))
    least = 1 if total - largest >= number_of - 1 else 0
    holding, spare = [largest] + [least] * (number_of - 1), total - largest - least * (number_of - 1)
    while spare > 0:
        free = [i for i in range(1, number_of) if holding[i] < largest] or [i for i in range(1, number_of) if holding[i] < most]
        whole, left = sum([loads[i] for i in free]), spare
        for i in free:
            extra = min(most - holding[i], max(1, left * loads[i] // whole), spare)
            holding[i] = holding[i] + extra
            spare = spare - extra
    return np.array(holding)


def scatter_about(key, shape, spread, reach, pieces=(), held_as=jnp.bfloat16):
    entries = spread * jax.random.normal(key, shape, jnp.float32)
    if pieces:
        entries = entries * steps_of(key, shape, pieces, -0.22, 0.18)
    return jnp.clip(entries, -reach, reach).astype(held_as)


def setup_inputs(seed: int = 0) -> dict:
    keys = jax.random.split(jax.random.key(seed), 8)
    tokens = scatter_about(keys[0], (TOKENS, D), 1.0, 6.0, ((0, 512),))
    cotangent = scatter_about(keys[1], (TOKENS, D), 1.0, 6.0, ((0, 512),))
    routing_keys = jax.random.split(jax.random.fold_in(keys[2], 1), TOKENS // TOK_DEV)
    routing_turns = jax.random.permutation(jax.random.fold_in(keys[2], 3), TOKENS // TOK_DEV)
    routing = jax.vmap(lambda own, number: assign_block(jax.random.fold_in(keys[2], 2), own, number, TOK_DEV, EXPERTS, TOP, CAP, 2))(routing_keys, routing_turns).reshape((TOKENS, TOP))
    gates = jnp.clip(0.049804688 + 0.9501953 * jax.random.uniform(keys[3], (TOKENS, TOP), jnp.float32) ** steps_of(keys[3], (TOKENS, TOP), ((0, 512),), -0.2, 0.2), 0.049804688, 1.0).astype(jnp.bfloat16)
    gate_weight = scatter_about(keys[4], (EXPERTS, D, F), D ** -0.5, 0.1875, ((0, 16),))
    up_weight = scatter_about(keys[5], (EXPERTS, D, F), D ** -0.5, 0.1875, ((0, 16),))
    down_weight = scatter_about(keys[6], (EXPERTS, F, D), F ** -0.5, 0.375, ((0, 16),))
    return dict(tokens=tokens, cotangent=cotangent, routing=routing, gates=gates, gate_weight=gate_weight, up_weight=up_weight, down_weight=down_weight)


def expert_pass(x_rows, dy_rows, g_rows, w_gate, w_up, w_down):
    pre_gate = jnp.dot(x_rows, w_gate, preferred_element_type=jnp.float32)
    pre_up = jnp.dot(x_rows, w_up, preferred_element_type=jnp.float32)
    sigmoid_gate = jax.nn.sigmoid(pre_gate)
    silu_gate = pre_gate * sigmoid_gate
    activated = (silu_gate * pre_up).astype(jnp.bfloat16)
    expert_out = jnp.dot(activated, w_down, preferred_element_type=jnp.float32)
    gate_terms = jnp.sum(dy_rows.astype(jnp.float32) * expert_out, axis=-1).astype(jnp.bfloat16)
    out_grad = (g_rows.astype(jnp.float32)[:, None] * dy_rows.astype(jnp.float32)).astype(jnp.bfloat16)
    act_grad = jnp.dot(out_grad, w_down.T, preferred_element_type=jnp.float32)
    down_term = jnp.dot(activated.T, out_grad, preferred_element_type=jnp.float32)
    gate_pre_grad = (act_grad * pre_up * sigmoid_gate * (1.0 + pre_gate * (1.0 - sigmoid_gate))).astype(jnp.bfloat16)
    up_pre_grad = (act_grad * silu_gate).astype(jnp.bfloat16)
    input_grad = (jnp.dot(gate_pre_grad, w_gate.T, preferred_element_type=jnp.float32)
                  + jnp.dot(up_pre_grad, w_up.T, preferred_element_type=jnp.float32)).astype(jnp.bfloat16)
    gate_term = jnp.dot(x_rows.T, gate_pre_grad, preferred_element_type=jnp.float32)
    up_term = jnp.dot(x_rows.T, up_pre_grad, preferred_element_type=jnp.float32)
    return input_grad, gate_terms, gate_term, up_term, down_term


def reference(tokens, cotangent, routing, gates, gate_weight, up_weight, down_weight):
    group_rows = N_EXPERT * TOK_DEV
    copy_count = TOK_DEV * TOP
    token_groups = tokens.reshape(N_DP, group_rows, D)
    cot_groups = cotangent.reshape(N_DP, group_rows, D)
    gate_groups = gates.reshape(N_DP, group_rows * TOP)
    route_blocks = routing.reshape(N_DP, N_EXPERT, copy_count)
    onehot = (route_blocks[..., None] == jnp.arange(EXPERTS, dtype=jnp.int32)).astype(jnp.int32)
    slot_index = jnp.sum((jnp.cumsum(onehot, axis=2) - 1) * onehot, axis=-1)
    source_ids = jnp.arange(N_EXPERT, dtype=jnp.int32)[None, :, None]
    replica_ids = jnp.arange(N_DP, dtype=jnp.int32)[:, None, None]
    position = ((replica_ids * EXPERTS + route_blocks) * N_EXPERT + source_ids) * CAP + slot_index
    copy_ids = source_ids * copy_count + jnp.arange(copy_count, dtype=jnp.int32)[None, None, :]
    copy_ids = jnp.broadcast_to(copy_ids, position.shape)
    table = jnp.zeros((N_DP * EXPERTS * N_EXPERT * CAP,), jnp.int32)
    table = table.at[position.reshape(-1)].set(copy_ids.reshape(-1) + 1) - 1
    table = table.reshape(N_DP, EXPERTS, N_EXPERT * CAP)

    def per_expert(carry, expert_id):
        w_gate = gate_weight[expert_id]
        w_up = up_weight[expert_id]
        w_down = down_weight[expert_id]

        def per_replica(inner, replica):
            grad_acc, terms_acc, sum_gate, sum_up, sum_down = inner
            entry = table[replica, expert_id]
            is_valid = entry >= 0
            copy_pick = jnp.maximum(entry, 0)
            token_index = copy_pick // TOP
            x_rows = jnp.where(is_valid[:, None], token_groups[replica][token_index], 0).astype(jnp.bfloat16)
            dy_rows = jnp.where(is_valid[:, None], cot_groups[replica][token_index], 0).astype(jnp.bfloat16)
            g_rows = jnp.where(is_valid, gate_groups[replica][copy_pick], 0).astype(jnp.bfloat16)
            input_grad, gate_terms, gate_term, up_term, down_term = expert_pass(x_rows, dy_rows, g_rows, w_gate, w_up, w_down)
            grad_acc = grad_acc.at[replica, token_index].add(jnp.where(is_valid[:, None], input_grad.astype(jnp.float32), 0.0))
            drop_index = jnp.where(is_valid, copy_pick, group_rows * TOP)
            terms_acc = terms_acc.at[replica, drop_index].set(gate_terms, mode="drop")
            sum_gate = sum_gate + gate_term.astype(jnp.bfloat16).astype(jnp.float32)
            sum_up = sum_up + up_term.astype(jnp.bfloat16).astype(jnp.float32)
            sum_down = sum_down + down_term.astype(jnp.bfloat16).astype(jnp.float32)
            return (grad_acc, terms_acc, sum_gate, sum_up, sum_down), None

        start = (carry[0], carry[1], jnp.zeros((D, F), jnp.float32), jnp.zeros((D, F), jnp.float32), jnp.zeros((F, D), jnp.float32))
        result, unused = lax.scan(per_replica, start, jnp.arange(N_DP, dtype=jnp.int32))
        return (result[0], result[1]), (result[2], result[3], result[4])

    begin = (jnp.zeros((N_DP, group_rows, D), jnp.float32), jnp.zeros((N_DP, group_rows * TOP), jnp.bfloat16))
    final, stacked = lax.scan(per_expert, begin, jnp.arange(EXPERTS, dtype=jnp.int32))
    token_grad = final[0].reshape(TOKENS, D).astype(jnp.bfloat16)
    gate_grad = final[1].reshape(TOKENS, TOP)
    return token_grad, gate_grad, stacked[0], stacked[1], stacked[2]
```

```python
import jax
import jax.numpy as jnp
from jax import lax
from jax.sharding import PartitionSpec as P

BF = jnp.bfloat16
F32 = jnp.float32


def matmul(a, b, dims):
    return lax.dot_general(a, b, (dims, ((), ())), preferred_element_type=F32)


def on_device(tokens, cotangent, routing, gates, gate_weight, up_weight, down_weight):
    groups = lax.axis_size("expert")
    replicas = lax.axis_size("dp")
    rows, width = tokens.shape
    w_gate, w_up, w_down = gate_weight[0], up_weight[0], down_weight[0]
    hidden = w_gate.shape[1]

    chosen = routing[:, :, None] == jnp.arange(groups, dtype=jnp.int32)
    dense_gates = jnp.sum(jnp.where(chosen, gates[:, :, None].astype(F32), 0.0), axis=1).T.astype(BF)

    all_x = lax.all_gather(tokens, "expert", axis=0, tiled=True)
    all_dy = lax.all_gather(cotangent, "expert", axis=0, tiled=True)
    own_gates = lax.all_to_all(dense_gates, "expert", split_axis=0, concat_axis=0, tiled=True)
    g = own_gates.reshape(-1, 1).astype(F32)

    pre_gate = matmul(all_x, w_gate, ((1,), (0,)))
    pre_up = matmul(all_x, w_up, ((1,), (0,)))
    back = matmul(all_dy, w_down, ((1,), (1,)))
    sig = jax.nn.sigmoid(pre_gate)
    silu = pre_gate * sig
    act = silu * pre_up
    terms = jnp.sum(act * back, axis=1).astype(BF).reshape(groups, rows)
    act_gated = (g * act).astype(BF)
    act_grad = g * back
    gate_pre = (act_grad * pre_up * sig * (1.0 + pre_gate * (1.0 - sig))).astype(BF)
    up_pre = (act_grad * silu).astype(BF)
    input_grad = (
        matmul(gate_pre, w_gate, ((1,), (1,))) + matmul(up_pre, w_up, ((1,), (1,)))
    ).astype(BF)
    token_grad = lax.psum_scatter(input_grad, "expert", scatter_dimension=0, tiled=True)

    d_gate = matmul(all_x, gate_pre, ((0,), (0,))).astype(BF).reshape(replicas, -1, hidden)
    d_up = matmul(all_x, up_pre, ((0,), (0,))).astype(BF).reshape(replicas, -1, hidden)
    d_down = matmul(act_gated, all_dy, ((0,), (0,))).astype(BF)
    slab = hidden // replicas
    d_down = d_down.reshape(replicas, slab, width // hidden, hidden).swapaxes(1, 2)
    d_down = d_down.reshape(replicas, -1, hidden)
    parts = jnp.concatenate([d_gate, d_up, d_down], axis=1)
    parts = lax.all_to_all(parts, "dp", split_axis=0, concat_axis=0, tiled=True)
    total = jnp.sum(parts.astype(F32), axis=0)
    n = width // replicas
    sum_gate, sum_up = total[:n], total[n : 2 * n]
    sum_down = total[2 * n :].reshape(width // hidden, slab, hidden).swapaxes(0, 1).reshape(slab, width)

    back_terms = lax.all_to_all(terms, "expert", split_axis=0, concat_axis=0, tiled=True)
    picked = jnp.where(chosen, back_terms.T[:, None, :].astype(F32), 0.0)
    gate_grad = jnp.sum(picked, axis=2).astype(BF)
    return token_grad, gate_grad, sum_gate[None], sum_up[None], sum_down[None]


def solution(mesh):
    in_specs = (
        P(("dp", "expert"), None),
        P(("dp", "expert"), None),
        P(("dp", "expert"), None),
        P(("dp", "expert"), None),
        P("expert", None, None),
        P("expert", None, None),
        P("expert", None, None),
    )
    out_specs = (
        P(("dp", "expert"), None),
        P(("dp", "expert"), None),
        P("expert", "dp", None),
        P("expert", "dp", None),
        P("expert", "dp", None),
    )
    return jax.shard_map(
        on_device, mesh=mesh, in_specs=in_specs, out_specs=out_specs, check_vma=False
    )
```

```python
import functools

import jax
import jax.numpy as jnp
from jax import lax
from jax.experimental import pallas as pl
from jax.experimental.pallas import tpu as pltpu
from jax.sharding import PartitionSpec as P

BF = jnp.bfloat16
F32 = jnp.float32
LANES = 128


def dot(a, b, ca, cb):
    return lax.dot_general(a, b, (((ca,), (cb,)), ((), ())), preferred_element_type=F32)


def pack_kernel(routing, gates, tokens, cotangent, out):
    rows, width = tokens.shape
    out[:, :width] = tokens[...]
    out[:, width : 2 * width] = cotangent[...]
    expert = lax.broadcasted_iota(jnp.int32, (LANES, rows), 0)
    dense = jnp.zeros((LANES, rows), F32)
    named, gate = routing[...], gates[...].astype(F32)
    for k in range(routing.shape[0]):
        dense = jnp.where(expert == named[k : k + 1], gate[k : k + 1], dense)
    out[:, 2 * width :] = dense.T.astype(BF)


def finish_kernel(routing, p, q, r, token_grad, gate_grad):
    rows, width = token_grad.shape
    total = p[...].astype(F32) + q[...].astype(F32) + r[:rows].astype(F32)
    token_grad[...] = total[:, :width].astype(BF)
    terms = total[:, width:].T
    expert = lax.broadcasted_iota(jnp.int32, (LANES, rows), 0)
    named = routing[...]
    picked = [
        jnp.sum(jnp.where(expert == named[k : k + 1], terms, 0.0), axis=0, keepdims=True)
        for k in range(routing.shape[0])
    ]
    gate_grad[...] = jnp.concatenate(picked, axis=0).astype(BF)


def group_kernel(first, last, width, hidden, replicas, expert_ref, b0, b1, w_own, w_oth, *refs):
    if first:
        out_grad, out_a, out_b = refs
    else:
        acc_gu, acc_d, out_grad, out_a, out_b = refs
    mine = expert_ref[0]
    x = jnp.concatenate([b0[:, :width], b1[:, :width]], axis=0)
    dy = jnp.concatenate([b0[:, width : 2 * width], b1[:, width : 2 * width]], axis=0)
    dense = jnp.concatenate([b0[:, 2 * width :], b1[:, 2 * width :]], axis=0).astype(F32)
    lane = lax.broadcasted_iota(jnp.int32, dense.shape, 1)
    terms = jnp.zeros(dense.shape, F32)
    grad = jnp.zeros(x.shape, F32)
    grads, acts = [], []
    for j, w in enumerate((w_own, w_oth)):
        here = lane == (mine if j == 0 else mine + 1 - 2 * lax.rem(mine, 2))
        g = jnp.sum(jnp.where(here, dense, 0.0), axis=1, keepdims=True)
        pre = dot(x, w[:, : 2 * hidden], 1, 0)
        pre_gate, pre_up = pre[:, :hidden], pre[:, hidden:]
        back = dot(dy, w[:, 2 * hidden :], 1, 0)
        sig = jax.nn.sigmoid(pre_gate)
        silu = pre_gate * sig
        act = silu * pre_up
        terms = terms + jnp.where(here, jnp.sum(act * back, axis=1, keepdims=True), 0.0)
        act_grad = g * back
        gate_pre = (act_grad * pre_up * sig * (1.0 + pre_gate * (1.0 - sig))).astype(BF)
        up_pre = (act_grad * silu).astype(BF)
        both = jnp.concatenate([gate_pre, up_pre], axis=1)
        grads.append(both)
        acts.append((g * act).astype(BF))
        grad = grad + dot(both, w[:, : 2 * hidden], 1, 1)
    out_grad[:, :width] = grad.astype(BF)
    out_grad[:, width:] = terms.astype(BF)

    n, m, half = width // replicas, hidden // replicas, width // 2
    grads = jnp.concatenate(grads, axis=1)
    step = max(n, 2 * hidden)
    for r in range(0, width, step):
        rows = slice(r, r + step)
        d_gu = dot(x[:, rows], grads, 0, 0)
        if not first:
            d_gu = d_gu + acc_gu[rows, :]
        if last:
            d_gu, reps = d_gu.astype(BF), step // n
            to = slice(r // n, r // n + reps)
            out_a[to, :n, :] = d_gu[:, : 2 * hidden].reshape(reps, n, 2 * hidden)
            out_b[to, :n, :] = d_gu[:, 2 * hidden :].reshape(reps, n, 2 * hidden)
        else:
            out_a[rows, :] = d_gu
    for j, act in enumerate(acts):
        rows = slice(j * hidden, (j + 1) * hidden)
        d_down = dot(act, dy, 0, 0)
        if not first:
            d_down = d_down + acc_d[rows, :]
        if last:
            d_down = jnp.concatenate(
                [d_down[:, :half].reshape(replicas, m, half), d_down[:, half:].reshape(replicas, m, half)], axis=1
            )
            (out_b if j else out_a)[:, n:, :] = d_down.astype(BF)
        else:
            out_b[rows, :] = d_down


VMEM = pl.BlockSpec(memory_space=pltpu.VMEM)


def group(first, last, replicas, expert, blocks, weights, acc):
    rows = blocks[0].shape[0]
    width, packed = weights[0].shape
    hidden = packed // 3
    if last:
        n, m = width // replicas, hidden // replicas
        sums = [jax.ShapeDtypeStruct((replicas, n + 2 * m, 2 * hidden), BF)] * 2
    else:
        sums = [
            jax.ShapeDtypeStruct((width, 4 * hidden), F32),
            jax.ShapeDtypeStruct((2 * hidden, width), F32),
        ]
    flops = 2 * 2 * rows * width * hidden * 16
    return pl.pallas_call(
        functools.partial(group_kernel, first, last, width, hidden, replicas),
        out_shape=[jax.ShapeDtypeStruct((2 * rows, width + LANES), BF)] + sums,
        in_specs=[pl.BlockSpec(memory_space=pltpu.SMEM)] + [VMEM] * (4 + len(acc)),
        out_specs=[VMEM] * 3,
        input_output_aliases={} if first or last else {5: 1, 6: 2},
        compiler_params=pltpu.CompilerParams(vmem_limit_bytes=26 * 1024 * 1024),
        cost_estimate=pl.CostEstimate(flops=flops, bytes_accessed=16 * 1024 * 1024, transcendentals=0),
    )(expert, *blocks, *weights, *acc)


def after(a, *others):
    return lax.optimization_barrier((a, *others))[0]


def on_device(tokens, cotangent, routing, gates, gate_weight, up_weight, down_weight):
    groups = lax.axis_size("expert")
    replicas = lax.axis_size("dp")
    rows, width = tokens.shape
    hidden = gate_weight.shape[2]
    out = [(i, (i + 2 if i % 2 == 0 else i - 2) % groups) for i in range(groups)]
    home = [(b, a) for a, b in out]
    swap = [(i, i ^ 1) for i in range(groups)]
    cross = [(i, (i - 1 if i % 2 == 0 else i + 1) % groups) for i in range(groups)]
    uncross = [(b, a) for a, b in cross]

    def send(a, pairs):
        return lax.ppermute(a, "expert", pairs)

    own = pl.pallas_call(
        pack_kernel,
        out_shape=jax.ShapeDtypeStruct((rows, 2 * width + LANES), BF),
        in_specs=[VMEM] * 4,
        out_specs=VMEM,
        compiler_params=pltpu.CompilerParams(vmem_limit_bytes=8 * 1024 * 1024),
    )(routing.T, gates.T, tokens, cotangent)
    w_own = jnp.concatenate([gate_weight[0], up_weight[0], down_weight[0].T], axis=1)
    expert = lax.axis_index("expert").astype(jnp.int32).reshape(1)

    a1 = send(own, out)
    b1 = send(own, cross)
    w_oth = send(w_own, swap)
    weights = (w_own, w_oth)
    a2 = send(a1, out)
    g0, *acc = group(True, False, replicas, expert, (own, a1), weights, ())
    b2 = send(b1, out)
    a3 = send(a2, out)
    g1, *acc = group(False, False, replicas, expert, (b1, a2), weights, acc)
    b3 = send(after(b2, g0), out)
    a4 = send(after(a3, g1), out)
    g2, *acc = group(False, False, replicas, expert, (b2, a3), weights, acc)
    g3, mine, theirs = group(False, True, replicas, expert, (b3, a4), weights, acc)

    got = send(theirs, swap)
    parts = (mine.astype(F32) + got.astype(F32)).astype(BF)
    parts = lax.all_to_all(parts, "dp", split_axis=0, concat_axis=0, tiled=True)
    total = jnp.sum(parts.astype(F32), axis=0)
    n, m = width // replicas, hidden // replicas
    sum_gate, sum_up = total[:n, :hidden], total[:n, hidden:]
    sum_down = jnp.concatenate([total[n : n + m], total[n + m :]], axis=1)

    def add(p, q):
        return (p.astype(F32) + q.astype(F32)).astype(BF)

    b = send(g3[:rows], home)
    a = send(g3[rows:], home)
    b = send(add(b, g2[:rows]), home)
    a = send(add(a, g2[rows:]), home)
    b = send(add(b, g1[:rows]), uncross)
    a = send(add(a, g1[rows:]), home)
    a = send(add(a, g0[rows:]), home)
    token_grad, gate_grad = pl.pallas_call(
        finish_kernel,
        out_shape=[jax.ShapeDtypeStruct((rows, width), BF), jax.ShapeDtypeStruct(gates.shape[::-1], BF)],
        in_specs=[VMEM] * 4,
        out_specs=[VMEM] * 2,
        compiler_params=pltpu.CompilerParams(vmem_limit_bytes=8 * 1024 * 1024),
    )(routing.T, a, b, g0)
    return token_grad, gate_grad.T, sum_gate[None], sum_up[None], sum_down[None]


def solution(mesh):
    in_specs = (
        P(("dp", "expert"), None),
        P(("dp", "expert"), None),
        P(("dp", "expert"), None),
        P(("dp", "expert"), None),
        P("expert", None, None),
        P("expert", None, None),
        P("expert", None, None),
    )
    out_specs = (
        P(("dp", "expert"), None),
        P(("dp", "expert"), None),
        P("expert", "dp", None),
        P("expert", "dp", None),
        P("expert", "dp", None),
    )
    return jax.shard_map(
        on_device, mesh=mesh, in_specs=in_specs, out_specs=out_specs, check_vma=False
    )
```

```python
import functools

import jax
import jax.numpy as jnp
from jax import lax
from jax.experimental import pallas as pl
from jax.experimental.pallas import tpu as pltpu
from jax.sharding import PartitionSpec as P

BF = jnp.bfloat16
F32 = jnp.float32
LANES = 128


def dot(a, b, ca, cb):
    return lax.dot_general(a, b, (((ca,), (cb,)), ((), ())), preferred_element_type=F32)


def pack_kernel(routing, gates, tokens, cotangent, out, named_ref, gate_ref, sems):
    rows, width = tokens.shape
    small = [pltpu.make_async_copy(routing, named_ref, sems.at[0]), pltpu.make_async_copy(gates, gate_ref, sems.at[1])]
    large = [
        pltpu.make_async_copy(tokens, out.at[:, pl.ds(0, width)], sems.at[2]),
        pltpu.make_async_copy(cotangent, out.at[:, pl.ds(width, width)], sems.at[3]),
    ]
    for copy in small + large:
        copy.start()
    for copy in small:
        copy.wait()
    expert = lax.broadcasted_iota(jnp.int32, (LANES, rows), 0)
    dense = jnp.zeros((LANES, rows), F32)
    named, gate = named_ref[...], gate_ref[...].astype(F32)
    for k in range(routing.shape[0]):
        dense = jnp.where(expert == named[k : k + 1], gate[k : k + 1], dense)
    out[:, 2 * width :] = dense.T.astype(BF)
    for copy in large:
        copy.wait()


def pack_weights_kernel(gate, up, down, follows, out, sems):
    width, hidden = gate.shape[1:]
    copies = [
        pltpu.make_async_copy(gate.at[0], out.at[pl.ds(0, width), pl.ds(0, hidden)], sems.at[0]),
        pltpu.make_async_copy(up.at[0], out.at[pl.ds(0, width), pl.ds(hidden, hidden)], sems.at[1]),
        pltpu.make_async_copy(down.at[0, :, pl.ds(0, width // 2)], out.at[pl.ds(width, hidden)], sems.at[2]),
        pltpu.make_async_copy(down.at[0, :, pl.ds(width // 2, width // 2)], out.at[pl.ds(width + hidden, hidden)], sems.at[3]),
    ]
    for copy in copies:
        copy.start()
    for copy in copies:
        copy.wait()


def finish_kernel(routing, p, q, r, token_grad, gate_grad):
    rows, width = token_grad.shape
    total = p[...].astype(F32) + q[...].astype(F32) + r[:rows].astype(F32)
    token_grad[...] = total[:, :width].astype(BF)
    terms = total[:, width:].T
    expert = lax.broadcasted_iota(jnp.int32, (LANES, rows), 0)
    named = routing[...]
    picked = [
        jnp.sum(jnp.where(expert == named[k : k + 1], terms, 0.0), axis=0, keepdims=True)
        for k in range(routing.shape[0])
    ]
    gate_grad[...] = jnp.concatenate(picked, axis=0).astype(BF)


def group_kernel(first, last, width, hidden, replicas, expert_ref, b0, b1, w_own, w_oth, *refs):
    if first:
        out_grad, out_a, out_b = refs
    else:
        acc_gu, acc_d, out_grad, out_a, out_b = refs
    mine = expert_ref[0]
    half = width // 2
    x = jnp.concatenate([b0[:, :width], b1[:, :width]], axis=0)
    dy = jnp.concatenate([b0[:, width : 2 * width], b1[:, width : 2 * width]], axis=0)
    dense = jnp.concatenate([b0[:, 2 * width :], b1[:, 2 * width :]], axis=0).astype(F32)
    lane = lax.broadcasted_iota(jnp.int32, dense.shape, 1)
    terms = jnp.zeros(dense.shape, F32)
    grad = jnp.zeros(x.shape, F32)
    grads, acts = [], []
    for j, w in enumerate((w_own, w_oth)):
        here = lane == (mine if j == 0 else mine + 1 - 2 * lax.rem(mine, 2))
        g = jnp.sum(jnp.where(here, dense, 0.0), axis=1, keepdims=True)
        pre = dot(x, w[:width], 1, 0)
        pre_gate, pre_up = pre[:, :hidden], pre[:, hidden:]
        back = dot(dy[:, :half], w[width : width + hidden], 1, 1) + dot(dy[:, half:], w[width + hidden :], 1, 1)
        sig = jax.nn.sigmoid(pre_gate)
        silu = pre_gate * sig
        act = silu * pre_up
        terms = terms + jnp.where(here, jnp.sum(act * back, axis=1, keepdims=True), 0.0)
        act_grad = g * back
        gate_pre = (act_grad * pre_up * sig * (1.0 + pre_gate * (1.0 - sig))).astype(BF)
        up_pre = (act_grad * silu).astype(BF)
        both = jnp.concatenate([gate_pre, up_pre], axis=1)
        grads.append(both)
        acts.append((g * act).astype(BF))
        grad = grad + dot(both, w[:width], 1, 1)
    out_grad[:, :width] = grad.astype(BF)
    out_grad[:, width:] = terms.astype(BF)

    n, m = width // replicas, hidden // replicas
    grads = jnp.concatenate(grads, axis=1)
    step = max(n, 2 * hidden)
    for r in range(0, width, step):
        rows = slice(r, r + step)
        d_gu = dot(x[:, rows], grads, 0, 0)
        if not first:
            d_gu = d_gu + acc_gu[rows, :]
        if last:
            d_gu, reps = d_gu.astype(BF), step // n
            to = slice(r // n, r // n + reps)
            out_a[to, :n, :] = d_gu[:, : 2 * hidden].reshape(reps, n, 2 * hidden)
            out_b[to, :n, :] = d_gu[:, 2 * hidden :].reshape(reps, n, 2 * hidden)
        else:
            out_a[rows, :] = d_gu
    for j, act in enumerate(acts):
        rows = slice(j * hidden, (j + 1) * hidden)
        d_down = dot(act, dy, 0, 0)
        if not first:
            d_down = d_down + acc_d[rows, :]
        if last:
            d_down = jnp.concatenate(
                [d_down[:, :half].reshape(replicas, m, half), d_down[:, half:].reshape(replicas, m, half)], axis=1
            )
            (out_b if j else out_a)[:, n:, :] = d_down.astype(BF)
        else:
            out_b[rows, :] = d_down


VMEM = pl.BlockSpec(memory_space=pltpu.VMEM)


def group(first, last, replicas, expert, blocks, weights, acc):
    rows = blocks[0].shape[0]
    hidden = weights[0].shape[1] // 2
    width = weights[0].shape[0] - 2 * hidden
    if last:
        n, m = width // replicas, hidden // replicas
        sums = [jax.ShapeDtypeStruct((replicas, n + 2 * m, 2 * hidden), BF)] * 2
    else:
        sums = [
            jax.ShapeDtypeStruct((width, 4 * hidden), F32),
            jax.ShapeDtypeStruct((2 * hidden, width), F32),
        ]
    flops = 2 * 2 * rows * width * hidden * 16
    return pl.pallas_call(
        functools.partial(group_kernel, first, last, width, hidden, replicas),
        out_shape=[jax.ShapeDtypeStruct((2 * rows, width + LANES), BF)] + sums,
        in_specs=[pl.BlockSpec(memory_space=pltpu.SMEM)] + [VMEM] * (4 + len(acc)),
        out_specs=[VMEM] * 3,
        input_output_aliases={} if first or last else {5: 1, 6: 2},
        compiler_params=pltpu.CompilerParams(vmem_limit_bytes=26 * 1024 * 1024),
        cost_estimate=pl.CostEstimate(flops=flops, bytes_accessed=16 * 1024 * 1024, transcendentals=0),
    )(expert, *blocks, *weights, *acc)


def after(a, *others):
    return lax.optimization_barrier((a, *others))[0]


def on_device(tokens, cotangent, routing, gates, gate_weight, up_weight, down_weight):
    groups = lax.axis_size("expert")
    replicas = lax.axis_size("dp")
    rows, width = tokens.shape
    hidden = gate_weight.shape[2]
    out = [(i, (i + 2 if i % 2 == 0 else i - 2) % groups) for i in range(groups)]
    home = [(b, a) for a, b in out]
    home_two = [(i, (i - 4 if i % 2 == 0 else i + 4) % groups) for i in range(groups)]
    swap = [(i, i ^ 1) for i in range(groups)]
    cross = [(i, (i - 1 if i % 2 == 0 else i + 1) % groups) for i in range(groups)]
    uncross = [(b, a) for a, b in cross]

    def send(a, pairs):
        return lax.ppermute(a, "expert", pairs)

    in_hbm = pl.BlockSpec(memory_space=pltpu.HBM)
    own = pl.pallas_call(
        pack_kernel,
        out_shape=jax.ShapeDtypeStruct((rows, 2 * width + LANES), BF),
        in_specs=[in_hbm] * 4,
        out_specs=VMEM,
        scratch_shapes=[
            pltpu.VMEM(routing.shape[::-1], jnp.int32),
            pltpu.VMEM(gates.shape[::-1], BF),
            pltpu.SemaphoreType.DMA((4,)),
        ],
        compiler_params=pltpu.CompilerParams(vmem_limit_bytes=58 * 1024 * 1024),
    )(routing.T, gates.T, tokens, cotangent)
    expert = lax.axis_index("expert").astype(jnp.int32).reshape(1)

    a1 = send(own, out)
    b1 = send(own, cross)
    w_own = pl.pallas_call(
        pack_weights_kernel,
        out_shape=jax.ShapeDtypeStruct((width + 2 * hidden, 2 * hidden), BF),
        in_specs=[in_hbm] * 4,
        out_specs=VMEM,
        scratch_shapes=[pltpu.SemaphoreType.DMA((4,))],
        compiler_params=pltpu.CompilerParams(vmem_limit_bytes=58 * 1024 * 1024),
    )(gate_weight, up_weight, down_weight, own)
    w_oth = send(after(w_own, a1, b1), swap)
    weights = (w_own, w_oth)
    a2 = send(after(a1, b1), out)
    g0, *acc = group(True, False, replicas, expert, (own, a1), weights, ())
    b2 = send(b1, out)
    a3 = send(after(a2, g0), out)
    g1, *acc = group(False, False, replicas, expert, (b1, a2), weights, acc)
    b3 = send(b2, out)
    a4 = send(after(a3, g1), out)
    g2, *acc = group(False, False, replicas, expert, (b2, a3), weights, acc)
    far = send(g2[rows:], home)
    g3, mine, theirs = group(False, True, replicas, expert, (b3, a4), weights, acc)

    def add(*parts):
        return functools.reduce(lambda p, q: p + q, [p.astype(F32) for p in parts]).astype(BF)

    farthest = send(g3[rows:], home_two)
    b = send(g3[:rows], home)

    got = send(theirs, swap)
    parts = (mine.astype(F32) + got.astype(F32)).astype(BF)
    parts = lax.all_to_all(after(parts, farthest, b), "dp", split_axis=0, concat_axis=0, tiled=True)
    total = jnp.sum(parts.astype(F32), axis=0)
    n, m = width // replicas, hidden // replicas
    sum_gate, sum_up = total[:n, :hidden], total[:n, hidden:]
    sum_down = jnp.concatenate([total[n : n + m], total[n + m :]], axis=1)

    b = send(add(b, g2[:rows]), home)
    a = send(add(farthest, far, g1[rows:]), home)
    b = send(add(b, g1[:rows]), uncross)
    a = send(add(a, g0[rows:]), home)
    token_grad, gate_grad = pl.pallas_call(
        finish_kernel,
        out_shape=[jax.ShapeDtypeStruct((rows, width), BF), jax.ShapeDtypeStruct(gates.shape[::-1], BF)],
        in_specs=[VMEM] * 4,
        out_specs=[VMEM] * 2,
        compiler_params=pltpu.CompilerParams(vmem_limit_bytes=8 * 1024 * 1024),
    )(routing.T, a, b, g0)
    return token_grad, gate_grad.T, sum_gate[None], sum_up[None], sum_down[None]


def solution(mesh):
    in_specs = (
        P(("dp", "expert"), None),
        P(("dp", "expert"), None),
        P(("dp", "expert"), None),
        P(("dp", "expert"), None),
        P("expert", None, None),
        P("expert", None, None),
        P("expert", None, None),
    )
    out_specs = (
        P(("dp", "expert"), None),
        P(("dp", "expert"), None),
        P("expert", "dp", None),
        P("expert", "dp", None),
        P("expert", "dp", None),
    )
    return jax.shard_map(
        on_device, mesh=mesh, in_specs=in_specs, out_specs=out_specs, check_vma=False
    )
```

```python
import functools

import jax
import jax.numpy as jnp
from jax import lax
from jax.experimental import pallas as pl
from jax.experimental.pallas import tpu as pltpu
from jax.sharding import PartitionSpec as P

BF = jnp.bfloat16
F32 = jnp.float32
LANES = 128
HOP_FLOPS = 7_000_000_000


def dot(a, b, ca, cb):
    return lax.dot_general(a, b, (((ca,), (cb,)), ((), ())), preferred_element_type=F32)


def pack_kernel(routing, gates, tokens, cotangent, out, named_ref, gate_ref, sems):
    rows, width = tokens.shape
    small = [pltpu.make_async_copy(routing, named_ref, sems.at[0]), pltpu.make_async_copy(gates, gate_ref, sems.at[1])]
    large = [
        pltpu.make_async_copy(tokens, out.at[:, pl.ds(0, width)], sems.at[2]),
        pltpu.make_async_copy(cotangent, out.at[:, pl.ds(width, width)], sems.at[3]),
    ]
    for copy in small + large:
        copy.start()
    for copy in small:
        copy.wait()
    expert = lax.broadcasted_iota(jnp.int32, (LANES, rows), 0)
    dense = jnp.zeros((LANES, rows), F32)
    named, gate = named_ref[...], gate_ref[...].astype(F32)
    for k in range(routing.shape[0]):
        dense = jnp.where(expert == named[k : k + 1], gate[k : k + 1], dense)
    out[:, 2 * width :] = dense.T.astype(BF)
    for copy in large:
        copy.wait()


def finish_kernel(routing, p, q, r, token_grad, gate_grad):
    rows, width = token_grad.shape
    total = p[...].astype(F32) + q[...].astype(F32) + r[...].astype(F32)
    token_grad[...] = total[:, :width].astype(BF)
    terms = total[:, width:].T
    expert = lax.broadcasted_iota(jnp.int32, (LANES, rows), 0)
    named = routing[...]
    picked = [
        jnp.sum(jnp.where(expert == named[k : k + 1], terms, 0.0), axis=0, keepdims=True)
        for k in range(routing.shape[0])
    ]
    gate_grad[...] = jnp.concatenate(picked, axis=0).astype(BF)


def group_kernel(first, last, width, hidden, replicas, expert_ref, b0, b1, *refs):
    weights, refs = (refs[:3], refs[3:6]), refs[6:]
    if first:
        grad0, grad1, out_a, out_b = refs
    else:
        acc_gu, acc_d, grad0, grad1, out_a, out_b = refs
    mine = expert_ref[0]
    half = width // 2
    x = jnp.concatenate([b0[:, :width], b1[:, :width]], axis=0)
    dy = jnp.concatenate([b0[:, width : 2 * width], b1[:, width : 2 * width]], axis=0)
    dense = jnp.concatenate([b0[:, 2 * width :], b1[:, 2 * width :]], axis=0).astype(F32)
    lane = lax.broadcasted_iota(jnp.int32, dense.shape, 1)
    terms = jnp.zeros(dense.shape, F32)
    grad = jnp.zeros(x.shape, F32)
    grads, acts = [], []
    for j, (w_gate, w_up, w_down) in enumerate(weights):
        here = lane == (mine if j == 0 else mine + 1 - 2 * lax.rem(mine, 2))
        g = jnp.sum(jnp.where(here, dense, 0.0), axis=1, keepdims=True)
        pre_gate, pre_up = dot(x, w_gate[...], 1, 0), dot(x, w_up[...], 1, 0)
        back = dot(dy, w_down[...], 1, 1)
        sig = jax.nn.sigmoid(pre_gate)
        silu = pre_gate * sig
        act = silu * pre_up
        terms = terms + jnp.where(here, jnp.sum(act * back, axis=1, keepdims=True), 0.0)
        act_grad = g * back
        gate_pre = (act_grad * pre_up * sig * (1.0 + pre_gate * (1.0 - sig))).astype(BF)
        up_pre = (act_grad * silu).astype(BF)
        grads += [gate_pre, up_pre]
        acts.append((g * act).astype(BF))
        grad = grad + dot(gate_pre, w_gate[...], 1, 1) + dot(up_pre, w_up[...], 1, 1)
    block = b0.shape[0]
    for i, out in enumerate((grad0, grad1)):
        out[:, :width] = grad[i * block : (i + 1) * block].astype(BF)
        out[:, width:] = terms[i * block : (i + 1) * block].astype(BF)

    n, m = width // replicas, hidden // replicas
    grads = jnp.concatenate(grads, axis=1)
    step = max(n, 2 * hidden)
    for r in range(0, width, step):
        rows = slice(r, r + step)
        d_gu = dot(x[:, rows], grads, 0, 0)
        if not first:
            d_gu = d_gu + acc_gu[rows, :]
        if last:
            d_gu, reps = d_gu.astype(BF), step // n
            to = slice(r // n, r // n + reps)
            out_a[to, :n, :] = d_gu[:, : 2 * hidden].reshape(reps, n, 2 * hidden)
            out_b[to, :n, :] = d_gu[:, 2 * hidden :].reshape(reps, n, 2 * hidden)
        else:
            out_a[rows, :] = d_gu
    for j, act in enumerate(acts):
        rows = slice(j * hidden, (j + 1) * hidden)
        d_down = dot(act, dy, 0, 0)
        if not first:
            d_down = d_down + acc_d[rows, :]
        if last:
            d_down = jnp.concatenate(
                [d_down[:, :half].reshape(replicas, m, half), d_down[:, half:].reshape(replicas, m, half)], axis=1
            )
            (out_b if j else out_a)[:, n:, :] = d_down.astype(BF)
        else:
            out_b[rows, :] = d_down


VMEM = pl.BlockSpec(memory_space=pltpu.VMEM)


def group(first, last, replicas, expert, blocks, weights, acc):
    rows = blocks[0].shape[0]
    width, hidden = weights[0].shape
    if last:
        n, m = width // replicas, hidden // replicas
        sums = [jax.ShapeDtypeStruct((replicas, n + 2 * m, 2 * hidden), BF)] * 2
    else:
        sums = [
            jax.ShapeDtypeStruct((width, 4 * hidden), F32),
            jax.ShapeDtypeStruct((2 * hidden, width), F32),
        ]
    flops = 2 * 2 * rows * width * hidden * 16
    return pl.pallas_call(
        functools.partial(group_kernel, first, last, width, hidden, replicas),
        out_shape=[jax.ShapeDtypeStruct((rows, width + LANES), BF)] * 2 + sums,
        in_specs=[pl.BlockSpec(memory_space=pltpu.SMEM)] + [VMEM] * (8 + len(acc)),
        out_specs=[VMEM] * 4,
        input_output_aliases={} if first or last else {9: 2, 10: 3},
        compiler_params=pltpu.CompilerParams(vmem_limit_bytes=26 * 1024 * 1024),
        cost_estimate=pl.CostEstimate(flops=flops, bytes_accessed=16 * 1024 * 1024, transcendentals=0),
    )(expert, *blocks, *weights, *acc)


def add_kernel(p, q, out):
    out[...] = (p[...].astype(F32) + q[...].astype(F32)).astype(BF)


def add(p, q):
    return pl.pallas_call(
        add_kernel,
        out_shape=jax.ShapeDtypeStruct(p.shape, BF),
        in_specs=[VMEM] * 2,
        out_specs=VMEM,
        compiler_params=pltpu.CompilerParams(vmem_limit_bytes=8 * 1024 * 1024),
        cost_estimate=pl.CostEstimate(flops=HOP_FLOPS, bytes_accessed=3 * 2 * p.size, transcendentals=0),
    )(p, q)


def after(a, *others):
    return lax.optimization_barrier((a, *others))[0]


def on_device(tokens, cotangent, routing, gates, gate_weight, up_weight, down_weight):
    groups = lax.axis_size("expert")
    replicas = lax.axis_size("dp")
    rows, width = tokens.shape
    hidden = gate_weight.shape[2]
    out = [(i, (i + 2 if i % 2 == 0 else i - 2) % groups) for i in range(groups)]
    home = [(b, a) for a, b in out]
    swap = [(i, i ^ 1) for i in range(groups)]
    cross = [(i, (i - 1 if i % 2 == 0 else i + 1) % groups) for i in range(groups)]
    uncross = [(b, a) for a, b in cross]

    def send(a, pairs):
        return lax.ppermute(a, "expert", pairs)

    in_hbm = pl.BlockSpec(memory_space=pltpu.HBM)
    own = pl.pallas_call(
        pack_kernel,
        out_shape=jax.ShapeDtypeStruct((rows, 2 * width + LANES), BF),
        in_specs=[in_hbm] * 4,
        out_specs=VMEM,
        scratch_shapes=[
            pltpu.VMEM(routing.shape[::-1], jnp.int32),
            pltpu.VMEM(gates.shape[::-1], BF),
            pltpu.SemaphoreType.DMA((4,)),
        ],
        compiler_params=pltpu.CompilerParams(vmem_limit_bytes=58 * 1024 * 1024),
    )(routing.T, gates.T, tokens, cotangent)
    expert = lax.axis_index("expert").astype(jnp.int32).reshape(1)

    a1 = send(own, out)
    b1 = send(own, cross)
    weights = [gate_weight[0], up_weight[0], down_weight[0]]
    weights = weights + [send(w, swap) for w in weights]
    a2 = send(a1, out)
    g_own, g_a1, *acc = group(True, False, replicas, expert, (own, a1), weights, ())
    b2 = send(b1, out)
    a3 = send(after(a2, g_a1), out)
    g_b1, g_a2, *acc = group(False, False, replicas, expert, (b1, a2), weights, acc)
    b3 = send(b2, out)
    a4 = send(after(a3, g_a2), out)
    g_b2, g_a3, *acc = group(False, False, replicas, expert, (b2, a3), weights, acc)
    g_b3, g_a4, mine, theirs = group(False, True, replicas, expert, (b3, a4), weights, acc)

    b = send(g_b3, home)
    a = send(g_a4, home)

    got = send(theirs, swap)
    parts = (mine.astype(F32) + got.astype(F32)).astype(BF)
    parts = lax.all_to_all(parts, "dp", split_axis=0, concat_axis=0, tiled=True)
    total = jnp.sum(parts.astype(F32), axis=0)
    n, m = width // replicas, hidden // replicas
    sum_gate, sum_up = total[:n, :hidden], total[:n, hidden:]
    sum_down = jnp.concatenate([total[n : n + m], total[n + m :]], axis=1)

    b = send(add(b, g_b2), home)
    a = send(add(a, g_a3), home)
    b = send(add(b, g_b1), uncross)
    a = send(add(a, g_a2), home)
    a = send(add(a, g_a1), home)
    token_grad, gate_grad = pl.pallas_call(
        finish_kernel,
        out_shape=[jax.ShapeDtypeStruct((rows, width), BF), jax.ShapeDtypeStruct(gates.shape[::-1], BF)],
        in_specs=[VMEM] * 4,
        out_specs=[VMEM] * 2,
        compiler_params=pltpu.CompilerParams(vmem_limit_bytes=8 * 1024 * 1024),
    )(routing.T, a, b, g_own)
    return token_grad, gate_grad.T, sum_gate[None], sum_up[None], sum_down[None]


def solution(mesh):
    in_specs = (
        P(("dp", "expert"), None),
        P(("dp", "expert"), None),
        P(("dp", "expert"), None),
        P(("dp", "expert"), None),
        P("expert", None, None),
        P("expert", None, None),
        P("expert", None, None),
    )
    out_specs = (
        P(("dp", "expert"), None),
        P(("dp", "expert"), None),
        P("expert", "dp", None),
        P("expert", "dp", None),
        P("expert", "dp", None),
    )
    return jax.shard_map(
        on_device, mesh=mesh, in_specs=in_specs, out_specs=out_specs, check_vma=False
    )
```

```python
import functools

import jax
import jax.numpy as jnp
from jax import lax
from jax.experimental import pallas as pl
from jax.experimental.pallas import tpu as pltpu
from jax.sharding import PartitionSpec as P

BF = jnp.bfloat16
F32 = jnp.float32
LANES = 128
HOP_FLOPS = 7_000_000_000


def dot(a, b, ca, cb):
    return lax.dot_general(a, b, (((ca,), (cb,)), ((), ())), preferred_element_type=F32)


def pack_kernel(routing, gates, tokens, cotangent, out, named_ref, gate_ref, sems):
    rows, width = tokens.shape
    small = [pltpu.make_async_copy(routing, named_ref, sems.at[0]), pltpu.make_async_copy(gates, gate_ref, sems.at[1])]
    large = [
        pltpu.make_async_copy(tokens, out.at[:, pl.ds(0, width)], sems.at[2]),
        pltpu.make_async_copy(cotangent, out.at[:, pl.ds(width, width)], sems.at[3]),
    ]
    for copy in small + large:
        copy.start()
    for copy in small:
        copy.wait()
    expert = lax.broadcasted_iota(jnp.int32, (LANES, rows), 0)
    dense = jnp.zeros((LANES, rows), F32)
    named, gate = named_ref[...], gate_ref[...].astype(F32)
    for k in range(routing.shape[0]):
        dense = jnp.where(expert == named[k : k + 1], gate[k : k + 1], dense)
    out[:, 2 * width :] = dense.T.astype(BF)
    for copy in large:
        copy.wait()


def finish_kernel(routing, p, q, r, token_grad, gate_grad):
    rows, width = token_grad.shape
    total = p[...].astype(F32) + q[...].astype(F32) + r[...].astype(F32)
    token_grad[...] = total[:, :width].astype(BF)
    terms = total[:, width:].T
    expert = lax.broadcasted_iota(jnp.int32, (LANES, rows), 0)
    named = routing[...]
    picked = [
        jnp.sum(jnp.where(expert == named[k : k + 1], terms, 0.0), axis=0, keepdims=True)
        for k in range(routing.shape[0])
    ]
    gate_grad[...] = jnp.concatenate(picked, axis=0).astype(BF)


def group_kernel(first, last, width, hidden, replicas, n_blocks, expert_ref, *refs):
    blocks, refs = refs[:n_blocks], refs[n_blocks:]
    weights, refs = (refs[:3], refs[3:6]), refs[6:]
    if not first:
        (acc_gu, acc_d), refs = refs[:2], refs[2:]
    out_grads, (out_a, out_b) = refs[:n_blocks], refs[n_blocks:]
    mine = expert_ref[0]
    half = width // 2
    x = jnp.concatenate([b[:, :width] for b in blocks], axis=0)
    dy = jnp.concatenate([b[:, width : 2 * width] for b in blocks], axis=0)
    dense = jnp.concatenate([b[:, 2 * width :] for b in blocks], axis=0).astype(F32)
    lane = lax.broadcasted_iota(jnp.int32, dense.shape, 1)
    terms = jnp.zeros(dense.shape, F32)
    grad = jnp.zeros(x.shape, F32)
    grads, acts = [], []
    for j, (w_gate, w_up, w_down) in enumerate(weights):
        here = lane == (mine if j == 0 else mine + 1 - 2 * lax.rem(mine, 2))
        g = jnp.sum(jnp.where(here, dense, 0.0), axis=1, keepdims=True)
        pre_gate, pre_up = dot(x, w_gate[...], 1, 0), dot(x, w_up[...], 1, 0)
        back = dot(dy, w_down[...], 1, 1)
        sig = jax.nn.sigmoid(pre_gate)
        silu = pre_gate * sig
        act = silu * pre_up
        terms = terms + jnp.where(here, jnp.sum(act * back, axis=1, keepdims=True), 0.0)
        act_grad = g * back
        gate_pre = (act_grad * pre_up * sig * (1.0 + pre_gate * (1.0 - sig))).astype(BF)
        up_pre = (act_grad * silu).astype(BF)
        grads += [gate_pre, up_pre]
        acts.append((g * act).astype(BF))
        grad = grad + dot(gate_pre, w_gate[...], 1, 1) + dot(up_pre, w_up[...], 1, 1)
    block = blocks[0].shape[0]
    for i, out in enumerate(out_grads):
        out[:, :width] = grad[i * block : (i + 1) * block].astype(BF)
        out[:, width:] = terms[i * block : (i + 1) * block].astype(BF)

    n, m = width // replicas, hidden // replicas
    grads = jnp.concatenate(grads, axis=1)
    step = max(n, 2 * hidden)
    for r in range(0, width, step):
        rows = slice(r, r + step)
        d_gu = dot(x[:, rows], grads, 0, 0)
        if not first:
            d_gu = d_gu + acc_gu[rows, :]
        if last:
            d_gu, reps = d_gu.astype(BF), step // n
            to = slice(r // n, r // n + reps)
            out_a[to, :n, :] = d_gu[:, : 2 * hidden].reshape(reps, n, 2 * hidden)
            out_b[to, :n, :] = d_gu[:, 2 * hidden :].reshape(reps, n, 2 * hidden)
        else:
            out_a[rows, :] = d_gu
    for j, act in enumerate(acts):
        rows = slice(j * hidden, (j + 1) * hidden)
        d_down = dot(act, dy, 0, 0)
        if not first:
            d_down = d_down + acc_d[rows, :]
        if last:
            d_down = jnp.concatenate(
                [d_down[:, :half].reshape(replicas, m, half), d_down[:, half:].reshape(replicas, m, half)], axis=1
            )
            (out_b if j else out_a)[:, n:, :] = d_down.astype(BF)
        else:
            out_b[rows, :] = d_down


def sum_kernel(parts, gate, up, down):
    n, hidden = gate.shape[1:]
    m = down.shape[1]
    total = jnp.sum(parts[...].astype(F32), axis=0)
    gate[0], up[0] = total[:n, :hidden], total[:n, hidden:]
    down[0] = jnp.concatenate([total[n : n + m], total[n + m :]], axis=1)


VMEM = pl.BlockSpec(memory_space=pltpu.VMEM)


def group(first, last, replicas, expert, blocks, weights, acc):
    rows = blocks[0].shape[0]
    width, hidden = weights[0].shape
    if last:
        n, m = width // replicas, hidden // replicas
        sums = [jax.ShapeDtypeStruct((replicas, n + 2 * m, 2 * hidden), BF)] * 2
    else:
        sums = [
            jax.ShapeDtypeStruct((width, 4 * hidden), F32),
            jax.ShapeDtypeStruct((2 * hidden, width), F32),
        ]
    flops = 2 * len(blocks) * rows * width * hidden * 16
    return pl.pallas_call(
        functools.partial(group_kernel, first, last, width, hidden, replicas, len(blocks)),
        out_shape=[jax.ShapeDtypeStruct((rows, width + LANES), BF)] * len(blocks) + sums,
        in_specs=[pl.BlockSpec(memory_space=pltpu.SMEM)] + [VMEM] * (6 + len(blocks) + len(acc)),
        out_specs=[VMEM] * (2 + len(blocks)),
        input_output_aliases={} if first or last else {7 + len(blocks): len(blocks), 8 + len(blocks): len(blocks) + 1},
        compiler_params=pltpu.CompilerParams(vmem_limit_bytes=26 * 1024 * 1024),
        cost_estimate=pl.CostEstimate(flops=flops, bytes_accessed=16 * 1024 * 1024, transcendentals=0),
    )(expert, *blocks, *weights, *acc)


def add_kernel(p, q, out):
    out[...] = (p[...].astype(F32) + q[...].astype(F32)).astype(BF)


def add(p, q, flops=HOP_FLOPS):
    return pl.pallas_call(
        add_kernel,
        out_shape=jax.ShapeDtypeStruct(p.shape, BF),
        in_specs=[VMEM] * 2,
        out_specs=VMEM,
        compiler_params=pltpu.CompilerParams(vmem_limit_bytes=8 * 1024 * 1024),
        cost_estimate=pl.CostEstimate(flops=flops, bytes_accessed=3 * 2 * p.size, transcendentals=0),
    )(p, q)


def after(a, *others):
    return lax.optimization_barrier((a, *others))[0]


def on_device(tokens, cotangent, routing, gates, gate_weight, up_weight, down_weight):
    groups = lax.axis_size("expert")
    replicas = lax.axis_size("dp")
    rows, width = tokens.shape
    hidden = gate_weight.shape[2]
    out = [(i, (i + 2 if i % 2 == 0 else i - 2) % groups) for i in range(groups)]
    home = [(b, a) for a, b in out]
    swap = [(i, i ^ 1) for i in range(groups)]
    cross = [(i, (i - 1 if i % 2 == 0 else i + 1) % groups) for i in range(groups)]
    uncross = [(b, a) for a, b in cross]

    def send(a, pairs):
        return lax.ppermute(a, "expert", pairs)

    in_hbm = pl.BlockSpec(memory_space=pltpu.HBM)
    own = pl.pallas_call(
        pack_kernel,
        out_shape=jax.ShapeDtypeStruct((rows, 2 * width + LANES), BF),
        in_specs=[in_hbm] * 4,
        out_specs=VMEM,
        scratch_shapes=[
            pltpu.VMEM(routing.shape[::-1], jnp.int32),
            pltpu.VMEM(gates.shape[::-1], BF),
            pltpu.SemaphoreType.DMA((4,)),
        ],
        compiler_params=pltpu.CompilerParams(vmem_limit_bytes=58 * 1024 * 1024),
    )(routing.T, gates.T, tokens, cotangent)
    expert = lax.axis_index("expert").astype(jnp.int32).reshape(1)

    a1 = send(own, out)
    b1 = send(own, cross)
    weights = [gate_weight[0], up_weight[0], down_weight[0]]
    weights = weights + [send(w, swap) for w in weights]
    a2 = send(a1, out)
    g_own, g_a1, *acc = group(True, False, replicas, expert, (own, a1), weights, ())
    b2 = send(b1, out)
    a3 = send(after(a2, g_a1), out)
    g_b1, g_a2, *acc = group(False, False, replicas, expert, (b1, a2), weights, acc)
    b3 = send(b2, out)
    a4 = send(after(a3, g_a2), out)
    g_b2, g_a3, *acc = group(False, False, replicas, expert, (b2, a3), weights, acc)
    g_b3, *acc = group(False, False, replicas, expert, (b3,), weights, acc)
    g_a4, mine, theirs = group(False, True, replicas, expert, (a4,), weights, acc)

    b = send(g_b3, home)
    a = send(g_a4, home)

    got = send(theirs, swap)
    parts = (mine.astype(F32) + got.astype(F32)).astype(BF)
    parts = lax.all_to_all(parts, "dp", split_axis=0, concat_axis=0, tiled=True)
    slab = jax.ShapeDtypeStruct((1, width // replicas, hidden), F32)
    sums = pl.pallas_call(
        sum_kernel,
        out_shape=[slab, slab, jax.ShapeDtypeStruct((1, hidden // replicas, width), F32)],
        in_specs=[VMEM],
        out_specs=[VMEM] * 3,
        compiler_params=pltpu.CompilerParams(vmem_limit_bytes=8 * 1024 * 1024),
    )(parts)

    b = send(add(b, g_b2, HOP_FLOPS // 2), home)
    a = send(add(a, g_a3), home)
    b = send(add(b, g_b1, HOP_FLOPS // 2), uncross)
    a = send(add(a, g_a2), home)
    a = send(add(a, g_a1), home)
    token_grad, gate_grad = pl.pallas_call(
        finish_kernel,
        out_shape=[jax.ShapeDtypeStruct((rows, width), BF), jax.ShapeDtypeStruct(gates.shape[::-1], BF)],
        in_specs=[VMEM] * 4,
        out_specs=[VMEM] * 2,
        compiler_params=pltpu.CompilerParams(vmem_limit_bytes=8 * 1024 * 1024),
    )(routing.T, a, b, g_own)
    return token_grad, gate_grad.T, *sums


def solution(mesh):
    in_specs = (
        P(("dp", "expert"), None),
        P(("dp", "expert"), None),
        P(("dp", "expert"), None),
        P(("dp", "expert"), None),
        P("expert", None, None),
        P("expert", None, None),
        P("expert", None, None),
    )
    out_specs = (
        P(("dp", "expert"), None),
        P(("dp", "expert"), None),
        P("expert", "dp", None),
        P("expert", "dp", None),
        P("expert", "dp", None),
    )
    return jax.shard_map(
        on_device, mesh=mesh, in_specs=in_specs, out_specs=out_specs, check_vma=False
    )
```

```python
import functools

import jax
import jax.numpy as jnp
from jax import lax
from jax.experimental import pallas as pl
from jax.experimental.pallas import tpu as pltpu
from jax.sharding import PartitionSpec as P

BF = jnp.bfloat16
F32 = jnp.float32
LANES = 128
HOP_FLOPS = 5_000_000_000
SIDE_FLOPS = 2_500_000_000


def dot(a, b, ca, cb):
    return lax.dot_general(a, b, (((ca,), (cb,)), ((), ())), preferred_element_type=F32)


def pack_kernel(routing, gates, tokens, cotangent, out, named_ref, gate_ref, sems):
    rows, width = tokens.shape
    small = [pltpu.make_async_copy(routing, named_ref, sems.at[0]), pltpu.make_async_copy(gates, gate_ref, sems.at[1])]
    large = [
        pltpu.make_async_copy(tokens, out.at[:, pl.ds(0, width)], sems.at[2]),
        pltpu.make_async_copy(cotangent, out.at[:, pl.ds(width, width)], sems.at[3]),
    ]
    for copy in small + large:
        copy.start()
    for copy in small:
        copy.wait()
    expert = lax.broadcasted_iota(jnp.int32, (LANES, rows), 0)
    dense = jnp.zeros((LANES, rows), F32)
    named, gate = named_ref[...], gate_ref[...].astype(F32)
    for k in range(routing.shape[0]):
        dense = jnp.where(expert == named[k : k + 1], gate[k : k + 1], dense)
    out[:, 2 * width :] = dense.T.astype(BF)
    for copy in large:
        copy.wait()


def finish_kernel(routing, p, q, r, token_grad, gate_grad):
    rows, width = token_grad.shape
    total = p[...].astype(F32) + q[...].astype(F32) + r[...].astype(F32)
    token_grad[...] = total[:, :width].astype(BF)
    terms = total[:, width:].T
    expert = lax.broadcasted_iota(jnp.int32, (LANES, rows), 0)
    named = routing[...]
    picked = [
        jnp.sum(jnp.where(expert == named[k : k + 1], terms, 0.0), axis=0, keepdims=True)
        for k in range(routing.shape[0])
    ]
    gate_grad[...] = jnp.concatenate(picked, axis=0).astype(BF)


def split(blocks, width):
    x = jnp.concatenate([b[:, :width] for b in blocks], axis=0)
    dy = jnp.concatenate([b[:, width : 2 * width] for b in blocks], axis=0)
    dense = jnp.concatenate([b[:, 2 * width :] for b in blocks], axis=0).astype(F32)
    return x, dy, dense


def one_expert(x, dy, g, w_gate, w_up, w_down):
    pre_gate, pre_up = dot(x, w_gate[...], 1, 0), dot(x, w_up[...], 1, 0)
    back = dot(dy, w_down[...], 1, 1)
    sig = jax.nn.sigmoid(pre_gate)
    silu = pre_gate * sig
    act = silu * pre_up
    act_grad = g * back
    gate_pre = (act_grad * pre_up * sig * (1.0 + pre_gate * (1.0 - sig))).astype(BF)
    up_pre = (act_grad * silu).astype(BF)
    return gate_pre, up_pre, (g * act).astype(BF), jnp.sum(act * back, axis=1, keepdims=True)


def both_experts(blocks, weights, mine, out_grads):
    width = weights[0][0].shape[0]
    x, dy, dense = split(blocks, width)
    lane = lax.broadcasted_iota(jnp.int32, dense.shape, 1)
    terms = jnp.zeros(dense.shape, F32)
    grad = jnp.zeros(x.shape, F32)
    grads, acts = [], []
    for j, (w_gate, w_up, w_down) in enumerate(weights):
        here = lane == (mine if j == 0 else mine + 1 - 2 * lax.rem(mine, 2))
        g = jnp.sum(jnp.where(here, dense, 0.0), axis=1, keepdims=True)
        gate_pre, up_pre, act, term = one_expert(x, dy, g, w_gate, w_up, w_down)
        terms = terms + jnp.where(here, term, 0.0)
        grads += [gate_pre, up_pre]
        acts.append(act)
        grad = grad + dot(gate_pre, w_gate[...], 1, 1) + dot(up_pre, w_up[...], 1, 1)
    rows = blocks[0].shape[0]
    for i, out in enumerate(out_grads):
        out[:, :width] = grad[i * rows : (i + 1) * rows].astype(BF)
        out[:, width:] = terms[i * rows : (i + 1) * rows].astype(BF)
    return x, dy, grads, acts


def to_parts(out, d_gu, first_row):
    replicas, rows, wide = out.shape
    n = rows * 2 // 3
    reps = d_gu.shape[0] // n
    out[first_row // n : first_row // n + reps, :n, :] = d_gu.astype(BF).reshape(reps, n, wide)


def down_to_parts(out, d_down):
    replicas, rows, half = out.shape
    m = rows // 3 // 2
    pieces = [d_down[:, :half].reshape(replicas, m, half), d_down[:, half:].reshape(replicas, m, half)]
    out[:, rows - 2 * m :, :] = jnp.concatenate(pieces, axis=1).astype(BF)


def group_kernel(first, swap, n_blocks, expert_ref, *refs):
    blocks, refs = refs[:n_blocks], refs[n_blocks:]
    weights, refs = (refs[:3], refs[3:6]), refs[6:]
    if not first:
        (acc_gu, acc_d), refs = refs[:2], refs[2:]
    out_grads, outs = refs[:n_blocks], refs[n_blocks:]
    width, hidden = weights[0][0].shape
    x, dy, grads, acts = both_experts(blocks, weights, expert_ref[0], out_grads)
    grads = jnp.concatenate(grads, axis=1)
    for rows in steps(outs, swap, width, hidden):
        d_gu = dot(x[:, rows], grads, 0, 0)
        if not first:
            d_gu = d_gu + acc_gu[rows, :]
        if swap:
            outs[0][rows, :] = d_gu[:, : 2 * hidden]
            to_parts(outs[2], d_gu[:, 2 * hidden :], rows.start)
        else:
            outs[0][rows, :] = d_gu
    for j, act in enumerate(acts):
        rows = slice(j * hidden, (j + 1) * hidden)
        d_down = dot(act, dy, 0, 0)
        if not first:
            d_down = d_down + acc_d[rows, :]
        if swap and j == 1:
            down_to_parts(outs[2], d_down)
        else:
            outs[1][rows, :] = d_down


def steps(outs, swap, width, hidden):
    step = max(width // outs[2].shape[0], 2 * hidden) if swap else 2 * hidden
    return [slice(r, r + step) for r in range(0, width, step)]


def far_kernel(expert_ref, block, *refs):
    weights, (out_grad, out_pre, out_act) = (refs[:3], refs[3:6]), refs[6:]
    _, _, grads, acts = both_experts([block], weights, expert_ref[0], [out_grad])
    out_pre[...] = jnp.concatenate(grads[:2], axis=1)
    out_act[...] = acts[0]


def last_kernel(expert_ref, block, pre, act, theirs, w_gate, w_up, w_down, acc_gu, acc_d, early, out):
    width, hidden = w_gate.shape
    x, dy, dense = split([theirs], width)
    here = lax.broadcasted_iota(jnp.int32, dense.shape, 1) == expert_ref[0]
    g = jnp.sum(jnp.where(here, dense, 0.0), axis=1, keepdims=True)
    gate_pre, up_pre, gated, _ = one_expert(x, dy, g, w_gate, w_up, w_down)
    x = jnp.concatenate([block[:, :width], x], axis=0)
    dy = jnp.concatenate([block[:, width : 2 * width], dy], axis=0)
    grads = jnp.concatenate([pre[...], jnp.concatenate([gate_pre, up_pre], axis=1)], axis=0)
    gated = jnp.concatenate([act[...], gated], axis=0)
    replicas, rows, wide = out.shape
    n, m = width // replicas, hidden // replicas
    step = max(n, 2 * hidden)
    for r in range(0, width, step):
        partner = early[r // n : (r + step) // n, :n, :].reshape(step, wide).astype(F32)
        d_gu = dot(x[:, r : r + step], grads, 0, 0) + acc_gu[r : r + step, :] + partner
        to_parts(out, d_gu, r)
    down_to_parts(out, dot(gated, dy, 0, 0) + acc_d[...])
    out[:, n:, :] = (out[:, n:, :].astype(F32) + early[:, n:, :].astype(F32)).astype(BF)


def sum_kernel(parts, gate, up, down):
    n, hidden = gate.shape[1:]
    m = down.shape[1]
    total = jnp.sum(parts[...].astype(F32), axis=0)
    gate[0], up[0] = total[:n, :hidden], total[:n, hidden:]
    down[0] = jnp.concatenate([total[n : n + m], total[n + m :]], axis=1)


VMEM = pl.BlockSpec(memory_space=pltpu.VMEM)


def call(kernel, out_shape, expert, operands, aliases, flops):
    return pl.pallas_call(
        kernel,
        out_shape=out_shape,
        in_specs=[pl.BlockSpec(memory_space=pltpu.SMEM)] + [VMEM] * len(operands),
        out_specs=[VMEM] * len(out_shape),
        input_output_aliases=aliases,
        compiler_params=pltpu.CompilerParams(vmem_limit_bytes=26 * 1024 * 1024),
        cost_estimate=pl.CostEstimate(flops=flops, bytes_accessed=16 * 1024 * 1024, transcendentals=0),
    )(expert, *operands)


def group(expert, blocks, weights, acc, replicas=0):
    rows = blocks[0].shape[0]
    width, hidden = weights[0].shape
    own = 2 * hidden if replicas else 4 * hidden
    shapes = [jax.ShapeDtypeStruct((rows, width + LANES), BF)] * len(blocks) + [
        jax.ShapeDtypeStruct((width, own), F32),
        jax.ShapeDtypeStruct((own // 2, width), F32),
    ]
    if replicas:
        shapes.append(jax.ShapeDtypeStruct((replicas, (width + 2 * hidden) // replicas, 2 * hidden), BF))
    n = len(blocks)
    return call(
        functools.partial(group_kernel, not acc, bool(replicas), n),
        shapes,
        expert,
        (*blocks, *weights, *acc),
        {7 + n: n, 8 + n: n + 1} if acc and not replicas else {},
        2 * n * rows * width * hidden * 16,
    )


def add_kernel(p, q, out):
    out[...] = (p[...].astype(F32) + q[...].astype(F32)).astype(BF)


def add(p, q, flops=HOP_FLOPS):
    return pl.pallas_call(
        add_kernel,
        out_shape=jax.ShapeDtypeStruct(p.shape, BF),
        in_specs=[VMEM] * 2,
        out_specs=VMEM,
        compiler_params=pltpu.CompilerParams(vmem_limit_bytes=8 * 1024 * 1024),
        cost_estimate=pl.CostEstimate(flops=flops, bytes_accessed=3 * 2 * p.size, transcendentals=0),
    )(p, q)


def after(a, *others):
    return lax.optimization_barrier((a, *others))[0]


def on_device(tokens, cotangent, routing, gates, gate_weight, up_weight, down_weight):
    groups = lax.axis_size("expert")
    replicas = lax.axis_size("dp")
    rows, width = tokens.shape
    hidden = gate_weight.shape[2]
    out = [(i, (i + 2 if i % 2 == 0 else i - 2) % groups) for i in range(groups)]
    home = [(b, a) for a, b in out]
    swap = [(i, i ^ 1) for i in range(groups)]
    cross = [(i, (i - 1 if i % 2 == 0 else i + 1) % groups) for i in range(groups)]
    uncross = [(b, a) for a, b in cross]

    def send(a, pairs):
        return lax.ppermute(a, "expert", pairs)

    in_hbm = pl.BlockSpec(memory_space=pltpu.HBM)
    own = pl.pallas_call(
        pack_kernel,
        out_shape=jax.ShapeDtypeStruct((rows, 2 * width + LANES), BF),
        in_specs=[in_hbm] * 4,
        out_specs=VMEM,
        scratch_shapes=[
            pltpu.VMEM(routing.shape[::-1], jnp.int32),
            pltpu.VMEM(gates.shape[::-1], BF),
            pltpu.SemaphoreType.DMA((4,)),
        ],
        compiler_params=pltpu.CompilerParams(vmem_limit_bytes=58 * 1024 * 1024),
    )(routing.T, gates.T, tokens, cotangent)
    expert = lax.axis_index("expert").astype(jnp.int32).reshape(1)

    a1 = send(own, out)
    b1 = send(own, cross)
    weights = [gate_weight[0], up_weight[0], down_weight[0]]
    weights = weights + [send(w, swap) for w in weights]
    a2 = send(a1, out)
    g_own, g_a1, *acc = group(expert, (own, a1), weights, ())
    b2 = send(b1, out)
    a3 = send(after(a2, g_a1), out)
    g_b1, g_a2, *acc = group(expert, (b1, a2), weights, acc)
    b3 = send(b2, out)
    a4 = send(after(a3, g_a2), out)
    g_b2, g_a3, *acc = group(expert, (b2, a3), weights, acc)
    g_b3, *acc, early = group(expert, (b3,), weights, acc, replicas)
    early = send(after(early, a4), swap)
    theirs = send(a4, swap)
    g_a4, pre, act = call(
        far_kernel,
        [
            jax.ShapeDtypeStruct((rows, width + LANES), BF),
            jax.ShapeDtypeStruct((rows, 2 * hidden), BF),
            jax.ShapeDtypeStruct((rows, hidden), BF),
        ],
        expert,
        (a4, *weights),
        {},
        2 * rows * width * hidden * 10,
    )
    (parts,) = call(
        last_kernel,
        [jax.ShapeDtypeStruct(early.shape, BF)],
        expert,
        (a4, pre, act, theirs, *weights[:3], *acc, early),
        {},
        2 * rows * width * hidden * 9,
    )

    b = send(g_b3, home)
    a = send(g_a4, home)

    parts = lax.all_to_all(parts, "dp", split_axis=0, concat_axis=0, tiled=True)
    slab = jax.ShapeDtypeStruct((1, width // replicas, hidden), F32)
    sums = pl.pallas_call(
        sum_kernel,
        out_shape=[slab, slab, jax.ShapeDtypeStruct((1, hidden // replicas, width), F32)],
        in_specs=[VMEM],
        out_specs=[VMEM] * 3,
        compiler_params=pltpu.CompilerParams(vmem_limit_bytes=8 * 1024 * 1024),
    )(parts)

    b = send(add(b, g_b2, SIDE_FLOPS), home)
    a = send(add(a, g_a3), home)
    b = send(add(b, g_b1, SIDE_FLOPS), uncross)
    a = send(add(a, g_a2), home)
    a = send(add(a, g_a1), home)
    token_grad, gate_grad = pl.pallas_call(
        finish_kernel,
        out_shape=[jax.ShapeDtypeStruct((rows, width), BF), jax.ShapeDtypeStruct(gates.shape[::-1], BF)],
        in_specs=[VMEM] * 4,
        out_specs=[VMEM] * 2,
        compiler_params=pltpu.CompilerParams(vmem_limit_bytes=8 * 1024 * 1024),
    )(routing.T, a, b, g_own)
    return token_grad, gate_grad.T, *sums


def solution(mesh):
    in_specs = (
        P(("dp", "expert"), None),
        P(("dp", "expert"), None),
        P(("dp", "expert"), None),
        P(("dp", "expert"), None),
        P("expert", None, None),
        P("expert", None, None),
        P("expert", None, None),
    )
    out_specs = (
        P(("dp", "expert"), None),
        P(("dp", "expert"), None),
        P("expert", "dp", None),
        P("expert", "dp", None),
        P("expert", "dp", None),
    )
    return jax.shard_map(
        on_device, mesh=mesh, in_specs=in_specs, out_specs=out_specs, check_vma=False
    )
```

```python
import functools
import math

import jax
import jax.numpy as jnp
from jax import lax
from jax.experimental import pallas as pl
from jax.experimental.pallas import tpu as pltpu
from jax.sharding import PartitionSpec as P

BF = jnp.bfloat16
F32 = jnp.float32
LANES = 128
HOP_FLOPS = 1_000_000_000
SIDE_FLOPS = 500_000_000


def dot(a, b, ca, cb):
    return lax.dot_general(a, b, (((ca,), (cb,)), ((), ())), preferred_element_type=F32)


def pack_kernel(routing, gates, tokens, cotangent, out, named_ref, gate_ref, sems):
    rows, width = tokens.shape
    small = [pltpu.make_async_copy(routing, named_ref, sems.at[0]), pltpu.make_async_copy(gates, gate_ref, sems.at[1])]
    large = [
        pltpu.make_async_copy(tokens, out.at[:, pl.ds(0, width)], sems.at[2]),
        pltpu.make_async_copy(cotangent, out.at[:, pl.ds(width, width)], sems.at[3]),
    ]
    for copy in small + large:
        copy.start()
    for copy in small:
        copy.wait()
    expert = lax.broadcasted_iota(jnp.int32, (LANES, rows), 0)
    dense = jnp.zeros((LANES, rows), F32)
    named, gate = named_ref[...], gate_ref[...].astype(F32)
    for k in range(routing.shape[0]):
        dense = jnp.where(expert == named[k : k + 1], gate[k : k + 1], dense)
    out[:, 2 * width :] = dense.T.astype(BF)
    for copy in large:
        copy.wait()


def finish_kernel(routing, p, q, r, token_grad, gate_grad):
    rows, width = token_grad.shape
    total = p[...].astype(F32) + q[...].astype(F32) + r[...].astype(F32)
    token_grad[...] = total[:, :width].astype(BF)
    terms = total[:, width:].T
    expert = lax.broadcasted_iota(jnp.int32, (LANES, rows), 0)
    named = routing[...]
    picked = [
        jnp.sum(jnp.where(expert == named[k : k + 1], terms, 0.0), axis=0, keepdims=True)
        for k in range(routing.shape[0])
    ]
    gate_grad[...] = jnp.concatenate(picked, axis=0).astype(BF)


def split(blocks, width):
    x = jnp.concatenate([b[:, :width] for b in blocks], axis=0)
    dy = jnp.concatenate([b[:, width : 2 * width] for b in blocks], axis=0)
    dense = jnp.concatenate([b[:, 2 * width :] for b in blocks], axis=0).astype(F32)
    return x, dy, dense


def one_expert(x, dy, g, w_gate, w_up, w_down):
    pre_gate, pre_up = dot(x, w_gate[...], 1, 0), dot(x, w_up[...], 1, 0)
    back = dot(dy, w_down[...], 1, 1)
    sig = jax.nn.sigmoid(pre_gate)
    silu = pre_gate * sig
    act = silu * pre_up
    act_grad = g * back
    gate_pre = (act_grad * pre_up * sig * (1.0 + pre_gate * (1.0 - sig))).astype(BF)
    up_pre = (act_grad * silu).astype(BF)
    return gate_pre, up_pre, (g * act).astype(BF), jnp.sum(act * back, axis=1, keepdims=True)


def both_experts(blocks, weights, mine, out_grads):
    width = weights[0][0].shape[0]
    x, dy, dense = split(blocks, width)
    lane = lax.broadcasted_iota(jnp.int32, dense.shape, 1)
    terms = jnp.zeros(dense.shape, F32)
    grad = jnp.zeros(x.shape, F32)
    grads, acts = [], []
    for j, (w_gate, w_up, w_down) in enumerate(weights):
        here = lane == (mine if j == 0 else mine + 1 - 2 * lax.rem(mine, 2))
        g = jnp.sum(jnp.where(here, dense, 0.0), axis=1, keepdims=True)
        gate_pre, up_pre, act, term = one_expert(x, dy, g, w_gate, w_up, w_down)
        terms = terms + jnp.where(here, term, 0.0)
        grads += [gate_pre, up_pre]
        acts.append(act)
        grad = grad + dot(gate_pre, w_gate[...], 1, 1) + dot(up_pre, w_up[...], 1, 1)
    rows = blocks[0].shape[0]
    for i, out in enumerate(out_grads):
        out[:, :width] = grad[i * rows : (i + 1) * rows].astype(BF)
        out[:, width:] = terms[i * rows : (i + 1) * rows].astype(BF)
    return x, dy, grads, acts


def to_parts(out, d_gu, first_row):
    nx, _, rows, wide = out.shape
    n = rows * 2 // 3
    y, ys = first_row // (nx * n), d_gu.shape[0] // (nx * n)
    pieces = d_gu.astype(BF).reshape(ys, nx, n, wide)
    for x in range(nx):
        out[x, y : y + ys, :n, :] = pieces[:, x]


def down_to_parts(out, d_down, early=None):
    nx, ny, rows, half = out.shape
    m = rows // 3 // 2
    pieces = [d_down[:, c : c + half].reshape(ny, nx, m, half) for c in (0, half)]
    pieces = jnp.concatenate(pieces, axis=2)
    for x in range(nx):
        piece = pieces[:, x]
        if early is not None:
            piece = piece + early[x, :, rows - 2 * m :, :].astype(F32)
        out[x, :, rows - 2 * m :, :] = piece.astype(BF)


def group_kernel(first, swap, n_blocks, expert_ref, *refs):
    blocks, refs = refs[:n_blocks], refs[n_blocks:]
    weights, refs = (refs[:3], refs[3:6]), refs[6:]
    if not first:
        (acc_gu, acc_d), refs = refs[:2], refs[2:]
    out_grads, outs = refs[:n_blocks], refs[n_blocks:]
    width, hidden = weights[0][0].shape
    x, dy, grads, acts = both_experts(blocks, weights, expert_ref[0], out_grads)
    grads = jnp.concatenate(grads, axis=1)
    for rows in steps(outs, swap, width, hidden):
        d_gu = dot(x[:, rows], grads, 0, 0)
        if not first:
            d_gu = d_gu + acc_gu[rows, :]
        if swap:
            outs[0][rows, :] = d_gu[:, : 2 * hidden]
            to_parts(outs[2], d_gu[:, 2 * hidden :], rows.start)
        else:
            outs[0][rows, :] = d_gu
    for j, act in enumerate(acts):
        rows = slice(j * hidden, (j + 1) * hidden)
        d_down = dot(act, dy, 0, 0)
        if not first:
            d_down = d_down + acc_d[rows, :]
        if swap and j == 1:
            down_to_parts(outs[2], d_down)
        else:
            outs[1][rows, :] = d_down


def steps(outs, swap, width, hidden):
    step = max(width // outs[2].shape[1], 2 * hidden) if swap else 2 * hidden
    return [slice(r, r + step) for r in range(0, width, step)]


def far_kernel(expert_ref, block, *refs):
    weights, (out_grad, out_pre, out_act) = (refs[:3], refs[3:6]), refs[6:]
    _, _, grads, acts = both_experts([block], weights, expert_ref[0], [out_grad])
    out_pre[...] = jnp.concatenate(grads[:2], axis=1)
    out_act[...] = acts[0]


def last_kernel(expert_ref, block, pre, act, theirs, w_gate, w_up, w_down, acc_gu, acc_d, early, out, made, sems):
    width, hidden = w_gate.shape
    x, dy, dense = split([theirs], width)
    here = lax.broadcasted_iota(jnp.int32, dense.shape, 1) == expert_ref[0]
    g = jnp.sum(jnp.where(here, dense, 0.0), axis=1, keepdims=True)
    gate_pre, up_pre, gated, _ = one_expert(x, dy, g, w_gate, w_up, w_down)
    x = jnp.concatenate([block[:, :width], x], axis=0)
    dy = jnp.concatenate([block[:, width : 2 * width], dy], axis=0)
    grads = jnp.concatenate([pre[...], jnp.concatenate([gate_pre, up_pre], axis=1)], axis=0)
    gated = jnp.concatenate([act[...], gated], axis=0)
    nx, ny, rows, wide = out.shape
    n = rows * 2 // 3
    step = max(nx * n, 2 * hidden)
    copies = []

    def leave(*where):
        copies.append(pltpu.make_async_copy(made.at[where], out.at[where], sems.at[len(copies)]))
        copies[-1].start()

    for r in range(0, width, step):
        y, ys = r // (nx * n), step // (nx * n)
        partner = jnp.stack([early[p, y : y + ys, :n, :] for p in range(nx)], axis=1)
        d_gu = dot(x[:, r : r + step], grads, 0, 0) + acc_gu[r : r + step, :]
        to_parts(made, d_gu + partner.reshape(step, wide).astype(F32), r)
        leave(slice(None), pl.ds(y, ys), pl.ds(0, n))
    down_to_parts(made, dot(gated, dy, 0, 0) + acc_d[...], early)
    leave(slice(None), slice(None), pl.ds(n, rows - n))
    for copy in copies:
        copy.wait()


def halfway_kernel(parts, out):
    out[...] = jnp.sum(parts[...].astype(F32), axis=0).astype(BF)


def sum_kernel(parts, gate, up, down):
    n, hidden = gate.shape[1:]
    m = down.shape[1]
    total = jnp.sum(parts[...].astype(F32), axis=0)
    gate[0], up[0] = total[:n, :hidden], total[:n, hidden:]
    down[0] = jnp.concatenate([total[n : n + m], total[n + m :]], axis=1)


VMEM = pl.BlockSpec(memory_space=pltpu.VMEM)


def call(kernel, out_shape, expert, operands, aliases, flops, out_specs=VMEM, scratch=()):
    return pl.pallas_call(
        kernel,
        out_shape=out_shape,
        in_specs=[pl.BlockSpec(memory_space=pltpu.SMEM)] + [VMEM] * len(operands),
        out_specs=[out_specs] * len(out_shape),
        scratch_shapes=scratch,
        input_output_aliases=aliases,
        compiler_params=pltpu.CompilerParams(vmem_limit_bytes=26 * 1024 * 1024),
        cost_estimate=pl.CostEstimate(flops=flops, bytes_accessed=16 * 1024 * 1024, transcendentals=0),
    )(expert, *operands)


def group(expert, blocks, weights, acc, replicas=()):
    rows = blocks[0].shape[0]
    width, hidden = weights[0].shape
    own = 2 * hidden if replicas else 4 * hidden
    shapes = [jax.ShapeDtypeStruct((rows, width + LANES), BF)] * len(blocks) + [
        jax.ShapeDtypeStruct((width, own), F32),
        jax.ShapeDtypeStruct((own // 2, width), F32),
    ]
    if replicas:
        shapes.append(jax.ShapeDtypeStruct((*replicas, (width + 2 * hidden) // math.prod(replicas), 2 * hidden), BF))
    n = len(blocks)
    return call(
        functools.partial(group_kernel, not acc, bool(replicas), n),
        shapes,
        expert,
        (*blocks, *weights, *acc),
        {7 + n: n, 8 + n: n + 1} if acc and not replicas else {},
        2 * n * rows * width * hidden * 16,
    )


def add_kernel(p, q, out):
    out[...] = (p[...].astype(F32) + q[...].astype(F32)).astype(BF)


def add(p, q, flops=HOP_FLOPS):
    return pl.pallas_call(
        add_kernel,
        out_shape=jax.ShapeDtypeStruct(p.shape, BF),
        in_specs=[VMEM] * 2,
        out_specs=VMEM,
        compiler_params=pltpu.CompilerParams(vmem_limit_bytes=8 * 1024 * 1024),
        cost_estimate=pl.CostEstimate(flops=flops, bytes_accessed=3 * 2 * p.size, transcendentals=0),
    )(p, q)


def after(a, *others):
    return lax.optimization_barrier((a, *others))[0]


def on_device(tokens, cotangent, routing, gates, gate_weight, up_weight, down_weight):
    groups = lax.axis_size("expert")
    replicas = lax.axis_size("dp")
    nx = 4 if replicas % 4 == 0 else 1
    ny = replicas // nx
    along_x = [[y * nx + x for x in range(nx)] for y in range(ny)]
    along_y = [[y * nx + x for y in range(ny)] for x in range(nx)]
    rows, width = tokens.shape
    hidden = gate_weight.shape[2]
    out = [(i, (i + 2 if i % 2 == 0 else i - 2) % groups) for i in range(groups)]
    home = [(b, a) for a, b in out]
    swap = [(i, i ^ 1) for i in range(groups)]
    cross = [(i, (i - 1 if i % 2 == 0 else i + 1) % groups) for i in range(groups)]
    uncross = [(b, a) for a, b in cross]

    def send(a, pairs):
        return lax.ppermute(a, "expert", pairs)

    in_hbm = pl.BlockSpec(memory_space=pltpu.HBM)
    own = pl.pallas_call(
        pack_kernel,
        out_shape=jax.ShapeDtypeStruct((rows, 2 * width + LANES), BF),
        in_specs=[in_hbm] * 4,
        out_specs=VMEM,
        scratch_shapes=[
            pltpu.VMEM(routing.shape[::-1], jnp.int32),
            pltpu.VMEM(gates.shape[::-1], BF),
            pltpu.SemaphoreType.DMA((4,)),
        ],
        compiler_params=pltpu.CompilerParams(vmem_limit_bytes=58 * 1024 * 1024),
    )(routing.T, gates.T, tokens, cotangent)
    expert = lax.axis_index("expert").astype(jnp.int32).reshape(1)

    a1 = send(own, out)
    b1 = send(own, cross)
    weights = [gate_weight[0], up_weight[0], down_weight[0]]
    weights = weights + [send(w, swap) for w in weights]
    a2 = send(a1, out)
    g_own, g_a1, *acc = group(expert, (own, a1), weights, ())
    b2 = send(b1, out)
    a3 = send(after(a2, g_a1), out)
    g_b1, g_a2, *acc = group(expert, (b1, a2), weights, acc)
    b3 = send(b2, out)
    a4 = send(after(a3, g_a2), out)
    g_b2, g_a3, *acc = group(expert, (b2, a3), weights, acc)
    g_b3, *acc, early = group(expert, (b3,), weights, acc, (nx, ny))
    early = send(after(early, a4), swap)
    theirs = send(a4, swap)
    g_a4, pre, act = call(
        far_kernel,
        [
            jax.ShapeDtypeStruct((rows, width + LANES), BF),
            jax.ShapeDtypeStruct((rows, 2 * hidden), BF),
            jax.ShapeDtypeStruct((rows, hidden), BF),
        ],
        expert,
        (a4, *weights),
        {},
        2 * rows * width * hidden * 10,
    )
    (parts,) = call(
        last_kernel,
        [jax.ShapeDtypeStruct(early.shape, BF)],
        expert,
        (a4, pre, act, theirs, *weights[:3], *acc, early),
        {},
        2 * rows * width * hidden * 9,
        in_hbm,
        [pltpu.VMEM(early.shape, BF), pltpu.SemaphoreType.DMA((8,))],
    )

    b = send(g_b3, home)
    a = send(g_a4, home)

    if nx > 1:
        parts = lax.all_to_all(parts, "dp", split_axis=0, concat_axis=0, axis_index_groups=along_x, tiled=True)
    parts = pl.pallas_call(
        halfway_kernel,
        out_shape=jax.ShapeDtypeStruct(parts.shape[1:], BF),
        in_specs=[VMEM],
        out_specs=VMEM,
        compiler_params=pltpu.CompilerParams(vmem_limit_bytes=8 * 1024 * 1024),
    )(parts)
    if ny > 1:
        parts = lax.all_to_all(parts, "dp", split_axis=0, concat_axis=0, axis_index_groups=along_y, tiled=True)
    slab = jax.ShapeDtypeStruct((1, width // replicas, hidden), F32)
    sums = pl.pallas_call(
        sum_kernel,
        out_shape=[slab, slab, jax.ShapeDtypeStruct((1, hidden // replicas, width), F32)],
        in_specs=[VMEM],
        out_specs=[VMEM] * 3,
        compiler_params=pltpu.CompilerParams(vmem_limit_bytes=8 * 1024 * 1024),
    )(parts)

    b = send(add(b, g_b2, SIDE_FLOPS), home)
    a = send(add(a, g_a3), home)
    b = send(add(b, g_b1, SIDE_FLOPS), uncross)
    a = send(add(a, g_a2), home)
    a = send(add(a, g_a1), home)
    token_grad, gate_grad = pl.pallas_call(
        finish_kernel,
        out_shape=[jax.ShapeDtypeStruct((rows, width), BF), jax.ShapeDtypeStruct(gates.shape[::-1], BF)],
        in_specs=[VMEM] * 4,
        out_specs=[VMEM] * 2,
        compiler_params=pltpu.CompilerParams(vmem_limit_bytes=8 * 1024 * 1024),
    )(routing.T, a, b, g_own)
    return token_grad, gate_grad.T, *sums


def solution(mesh):
    in_specs = (
        P(("dp", "expert"), None),
        P(("dp", "expert"), None),
        P(("dp", "expert"), None),
        P(("dp", "expert"), None),
        P("expert", None, None),
        P("expert", None, None),
        P("expert", None, None),
    )
    out_specs = (
        P(("dp", "expert"), None),
        P(("dp", "expert"), None),
        P("expert", "dp", None),
        P("expert", "dp", None),
        P("expert", "dp", None),
    )
    return jax.shard_map(
        on_device, mesh=mesh, in_specs=in_specs, out_specs=out_specs, check_vma=False
    )
```

```python
import functools
import math

import jax
import jax.numpy as jnp
from jax import lax
from jax.experimental import pallas as pl
from jax.experimental.pallas import tpu as pltpu
from jax.sharding import PartitionSpec as P

BF = jnp.bfloat16
F32 = jnp.float32
LANES = 128
HOP_FLOPS = 4_000_000_000
SIDE_FLOPS = 2_000_000_000


def dot(a, b, ca, cb):
    return lax.dot_general(a, b, (((ca,), (cb,)), ((), ())), preferred_element_type=F32)


def pack_kernel(routing, gates, tokens, cotangent, out, named_ref, gate_ref, sems):
    rows, width = tokens.shape
    small = [pltpu.make_async_copy(routing, named_ref, sems.at[0]), pltpu.make_async_copy(gates, gate_ref, sems.at[1])]
    large = [
        pltpu.make_async_copy(tokens, out.at[:, pl.ds(0, width)], sems.at[2]),
        pltpu.make_async_copy(cotangent, out.at[:, pl.ds(width, width)], sems.at[3]),
    ]
    for copy in small + large:
        copy.start()
    for copy in small:
        copy.wait()
    expert = lax.broadcasted_iota(jnp.int32, (LANES, rows), 0)
    dense = jnp.zeros((LANES, rows), F32)
    named, gate = named_ref[...], gate_ref[...].astype(F32)
    for k in range(routing.shape[0]):
        dense = jnp.where(expert == named[k : k + 1], gate[k : k + 1], dense)
    out[:, 2 * width :] = dense.T.astype(BF)
    for copy in large:
        copy.wait()


def finish_kernel(routing, p, q, r, token_grad, gate_grad):
    rows, width = token_grad.shape
    total = p[...].astype(F32) + q[...].astype(F32) + r[...].astype(F32)
    token_grad[...] = total[:, :width].astype(BF)
    terms = total[:, width:].T
    expert = lax.broadcasted_iota(jnp.int32, (LANES, rows), 0)
    named = routing[...]
    picked = [
        jnp.sum(jnp.where(expert == named[k : k + 1], terms, 0.0), axis=0, keepdims=True)
        for k in range(routing.shape[0])
    ]
    gate_grad[...] = jnp.concatenate(picked, axis=0).astype(BF)


def split(blocks, width):
    x = jnp.concatenate([b[:, :width] for b in blocks], axis=0)
    dy = jnp.concatenate([b[:, width : 2 * width] for b in blocks], axis=0)
    dense = jnp.concatenate([b[:, 2 * width :] for b in blocks], axis=0).astype(F32)
    return x, dy, dense


def one_expert(x, dy, g, w_gate, w_up, w_down):
    pre_gate, pre_up = dot(x, w_gate[...], 1, 0), dot(x, w_up[...], 1, 0)
    back = dot(dy, w_down[...], 1, 1)
    sig = jax.nn.sigmoid(pre_gate)
    silu = pre_gate * sig
    act = silu * pre_up
    act_grad = g * back
    gate_pre = (act_grad * pre_up * sig * (1.0 + pre_gate * (1.0 - sig))).astype(BF)
    up_pre = (act_grad * silu).astype(BF)
    return gate_pre, up_pre, (g * act).astype(BF), jnp.sum(act * back, axis=1, keepdims=True)


def both_experts(blocks, weights, mine, out_grads):
    width = weights[0][0].shape[0]
    x, dy, dense = split(blocks, width)
    lane = lax.broadcasted_iota(jnp.int32, dense.shape, 1)
    terms = jnp.zeros(dense.shape, F32)
    grad = jnp.zeros(x.shape, F32)
    grads, acts = [], []
    for j, (w_gate, w_up, w_down) in enumerate(weights):
        here = lane == (mine if j == 0 else mine + 1 - 2 * lax.rem(mine, 2))
        g = jnp.sum(jnp.where(here, dense, 0.0), axis=1, keepdims=True)
        gate_pre, up_pre, act, term = one_expert(x, dy, g, w_gate, w_up, w_down)
        terms = terms + jnp.where(here, term, 0.0)
        grads += [gate_pre, up_pre]
        acts.append(act)
        grad = grad + dot(gate_pre, w_gate[...], 1, 1) + dot(up_pre, w_up[...], 1, 1)
    rows = blocks[0].shape[0]
    for i, out in enumerate(out_grads):
        out[:, :width] = grad[i * rows : (i + 1) * rows].astype(BF)
        out[:, width:] = terms[i * rows : (i + 1) * rows].astype(BF)
    return x, dy, grads, acts


def put(outs, where, value):
    at = 0
    for out in outs:
        wide = out.shape[-1]
        out[where] = value[..., at : at + wide]
        at += wide


def to_parts(outs, d_gu, first_row):
    nx, _, rows, _ = outs[0].shape
    n = rows * 2 // 3
    y, ys = first_row // (nx * n), d_gu.shape[0] // (nx * n)
    pieces = d_gu.astype(BF).reshape(ys, nx, n, d_gu.shape[1])
    for x in range(nx):
        put(outs, (x, slice(y, y + ys), slice(0, n)), pieces[:, x])


def down_to_parts(outs, d_down, early=()):
    nx, ny, rows, _ = outs[0].shape
    m, half = rows // 3 // 2, d_down.shape[1] // 2
    pieces = [d_down[:, c : c + half].reshape(ny, nx, m, half) for c in (0, half)]
    pieces = jnp.concatenate(pieces, axis=2)
    for x in range(nx):
        piece, where = pieces[:, x], (x, slice(0, ny), slice(rows - 2 * m, rows))
        if early:
            piece = piece + jnp.concatenate([e[where] for e in early], axis=-1).astype(F32)
        put(outs, where, piece.astype(BF))


def group_kernel(first, swap, n_blocks, expert_ref, *refs):
    blocks, refs = refs[:n_blocks], refs[n_blocks:]
    weights, refs = (refs[:3], refs[3:6]), refs[6:]
    if not first:
        (acc_gu, acc_d), refs = refs[:2], refs[2:]
    out_grads, outs = refs[:n_blocks], refs[n_blocks:]
    width, hidden = weights[0][0].shape
    x, dy, grads, acts = both_experts(blocks, weights, expert_ref[0], out_grads)
    grads = jnp.concatenate(grads, axis=1)
    for rows in steps(outs, swap, width, hidden):
        d_gu = dot(x[:, rows], grads, 0, 0)
        if not first:
            d_gu = d_gu + acc_gu[rows, :]
        if swap:
            outs[0][rows, :] = d_gu[:, : 2 * hidden]
            to_parts(outs[2:], d_gu[:, 2 * hidden :], rows.start)
        else:
            outs[0][rows, :] = d_gu
    for j, act in enumerate(acts):
        rows = slice(j * hidden, (j + 1) * hidden)
        d_down = dot(act, dy, 0, 0)
        if not first:
            d_down = d_down + acc_d[rows, :]
        if swap and j == 1:
            down_to_parts(outs[2:], d_down)
        else:
            outs[1][rows, :] = d_down


def steps(outs, swap, width, hidden):
    step = max(width // outs[2].shape[1], 2 * hidden) if swap else 2 * hidden
    return [slice(r, r + step) for r in range(0, width, step)]


def far_kernel(expert_ref, block, *refs):
    weights, (out_grad, out_pre, out_act) = (refs[:3], refs[3:6]), refs[6:]
    _, _, grads, acts = both_experts([block], weights, expert_ref[0], [out_grad])
    out_pre[...] = jnp.concatenate(grads[:2], axis=1)
    out_act[...] = acts[0]


def last_kernel(expert_ref, block, pre, act, theirs, w_gate, w_up, w_down, acc_gu, acc_d, *refs):
    *early, out, made, sems = refs
    width, hidden = w_gate.shape
    x, dy, dense = split([theirs], width)
    here = lax.broadcasted_iota(jnp.int32, dense.shape, 1) == expert_ref[0]
    g = jnp.sum(jnp.where(here, dense, 0.0), axis=1, keepdims=True)
    gate_pre, up_pre, gated, _ = one_expert(x, dy, g, w_gate, w_up, w_down)
    x = jnp.concatenate([block[:, :width], x], axis=0)
    dy = jnp.concatenate([block[:, width : 2 * width], dy], axis=0)
    grads = jnp.concatenate([pre[...], jnp.concatenate([gate_pre, up_pre], axis=1)], axis=0)
    gated = jnp.concatenate([act[...], gated], axis=0)
    nx, ny, rows, wide = out.shape
    n = rows * 2 // 3
    step = max(nx * n, 2 * hidden)
    copies = []

    def leave(*where):
        copies.append(pltpu.make_async_copy(made.at[where], out.at[where], sems.at[len(copies)]))
        copies[-1].start()

    for r in range(0, width, step):
        y, ys = r // (nx * n), step // (nx * n)
        partner = [jnp.stack([e[p, y : y + ys, :n, :] for p in range(nx)], axis=1) for e in early]
        partner = jnp.concatenate(partner, axis=-1)
        d_gu = dot(x[:, r : r + step], grads, 0, 0) + acc_gu[r : r + step, :]
        to_parts([made], d_gu + partner.reshape(step, wide).astype(F32), r)
        leave(slice(None), pl.ds(y, ys), pl.ds(0, n))
    down_to_parts([made], dot(gated, dy, 0, 0) + acc_d[...], early)
    leave(slice(None), slice(None), pl.ds(n, rows - n))
    for copy in copies:
        copy.wait()


def halfway_kernel(parts, out):
    out[...] = jnp.sum(parts[...].astype(F32), axis=0).astype(BF)


def sum_kernel(parts, gate, up, down):
    n, hidden = gate.shape[1:]
    m = down.shape[1]
    total = jnp.sum(parts[...].astype(F32), axis=0)
    gate[0], up[0] = total[:n, :hidden], total[:n, hidden:]
    down[0] = jnp.concatenate([total[n : n + m], total[n + m :]], axis=1)


VMEM = pl.BlockSpec(memory_space=pltpu.VMEM)


def call(kernel, out_shape, expert, operands, aliases, flops, out_specs=VMEM, scratch=()):
    return pl.pallas_call(
        kernel,
        out_shape=out_shape,
        in_specs=[pl.BlockSpec(memory_space=pltpu.SMEM)] + [VMEM] * len(operands),
        out_specs=[out_specs] * len(out_shape),
        scratch_shapes=scratch,
        input_output_aliases=aliases,
        compiler_params=pltpu.CompilerParams(vmem_limit_bytes=26 * 1024 * 1024),
        cost_estimate=pl.CostEstimate(flops=flops, bytes_accessed=16 * 1024 * 1024, transcendentals=0),
    )(expert, *operands)


def group(expert, blocks, weights, acc, replicas=()):
    rows = blocks[0].shape[0]
    width, hidden = weights[0].shape
    own = 2 * hidden if replicas else 4 * hidden
    shapes = [jax.ShapeDtypeStruct((rows, width + LANES), BF)] * len(blocks) + [
        jax.ShapeDtypeStruct((width, own), F32),
        jax.ShapeDtypeStruct((own // 2, width), F32),
    ]
    if replicas:
        shapes += [jax.ShapeDtypeStruct((*replicas, (width + 2 * hidden) // math.prod(replicas), hidden), BF)] * 2
    n = len(blocks)
    return call(
        functools.partial(group_kernel, not acc, bool(replicas), n),
        shapes,
        expert,
        (*blocks, *weights, *acc),
        {7 + n: n, 8 + n: n + 1} if acc and not replicas else {},
        2 * n * rows * width * hidden * 16,
    )


def add_kernel(p, q, out):
    out[...] = (p[...].astype(F32) + q[...].astype(F32)).astype(BF)


def add(p, q, flops=HOP_FLOPS):
    return pl.pallas_call(
        add_kernel,
        out_shape=jax.ShapeDtypeStruct(p.shape, BF),
        in_specs=[VMEM] * 2,
        out_specs=VMEM,
        compiler_params=pltpu.CompilerParams(vmem_limit_bytes=8 * 1024 * 1024),
        cost_estimate=pl.CostEstimate(flops=flops, bytes_accessed=3 * 2 * p.size, transcendentals=0),
    )(p, q)


def after(a, *others):
    return lax.optimization_barrier((a, *others))[0]


def on_device(tokens, cotangent, routing, gates, gate_weight, up_weight, down_weight):
    groups = lax.axis_size("expert")
    replicas = lax.axis_size("dp")
    nx = 4 if replicas % 4 == 0 else 1
    ny = replicas // nx
    along_x = [[y * nx + x for x in range(nx)] for y in range(ny)]
    along_y = [[y * nx + x for y in range(ny)] for x in range(nx)]
    rows, width = tokens.shape
    hidden = gate_weight.shape[2]
    out = [(i, (i + 2 if i % 2 == 0 else i - 2) % groups) for i in range(groups)]
    home = [(b, a) for a, b in out]
    swap = [(i, i ^ 1) for i in range(groups)]
    cross = [(i, (i - 1 if i % 2 == 0 else i + 1) % groups) for i in range(groups)]
    uncross = [(b, a) for a, b in cross]

    def send(a, pairs):
        return lax.ppermute(a, "expert", pairs)

    in_hbm = pl.BlockSpec(memory_space=pltpu.HBM)
    own = pl.pallas_call(
        pack_kernel,
        out_shape=jax.ShapeDtypeStruct((rows, 2 * width + LANES), BF),
        in_specs=[in_hbm] * 4,
        out_specs=VMEM,
        scratch_shapes=[
            pltpu.VMEM(routing.shape[::-1], jnp.int32),
            pltpu.VMEM(gates.shape[::-1], BF),
            pltpu.SemaphoreType.DMA((4,)),
        ],
        compiler_params=pltpu.CompilerParams(vmem_limit_bytes=58 * 1024 * 1024),
    )(routing.T, gates.T, tokens, cotangent)
    expert = lax.axis_index("expert").astype(jnp.int32).reshape(1)

    a1 = send(own, out)
    b1 = send(own, cross)
    weights = [gate_weight[0], up_weight[0], down_weight[0]]
    weights = weights + [send(w, swap) for w in weights]
    a2 = send(a1, out)
    g_own, g_a1, *acc = group(expert, (own, a1), weights, ())
    b2 = send(b1, out)
    a3 = send(after(a2, g_a1), out)
    g_b1, g_a2, *acc = group(expert, (b1, a2), weights, acc)
    b3 = send(b2, out)
    a4 = send(after(a3, g_a2), out)
    g_b2, g_a3, *acc = group(expert, (b2, a3), weights, acc)
    g_b3, *acc, early0, early1 = group(expert, (b3,), weights, acc, (nx, ny))
    early = [send(early0, swap), send(early1, swap)]
    whole = jax.ShapeDtypeStruct((*early0.shape[:-1], 2 * hidden), BF)
    theirs = send(a4, swap)
    g_a4, pre, act = call(
        far_kernel,
        [
            jax.ShapeDtypeStruct((rows, width + LANES), BF),
            jax.ShapeDtypeStruct((rows, 2 * hidden), BF),
            jax.ShapeDtypeStruct((rows, hidden), BF),
        ],
        expert,
        (a4, *weights),
        {},
        2 * rows * width * hidden * 10,
    )
    (parts,) = call(
        last_kernel,
        [whole],
        expert,
        (a4, pre, act, theirs, *weights[:3], *acc, *early),
        {},
        2 * rows * width * hidden * 9,
        in_hbm,
        [pltpu.VMEM(whole.shape, BF), pltpu.SemaphoreType.DMA((8,))],
    )

    b = send(g_b3, home)
    a = send(g_a4, home)

    if nx > 1:
        parts = lax.all_to_all(parts, "dp", split_axis=0, concat_axis=0, axis_index_groups=along_x, tiled=True)
    parts = pl.pallas_call(
        halfway_kernel,
        out_shape=jax.ShapeDtypeStruct(parts.shape[1:], BF),
        in_specs=[VMEM],
        out_specs=VMEM,
        compiler_params=pltpu.CompilerParams(vmem_limit_bytes=8 * 1024 * 1024),
    )(parts)
    if ny > 1:
        parts = lax.all_to_all(parts, "dp", split_axis=0, concat_axis=0, axis_index_groups=along_y, tiled=True)
    slab = jax.ShapeDtypeStruct((1, width // replicas, hidden), F32)
    sums = pl.pallas_call(
        sum_kernel,
        out_shape=[slab, slab, jax.ShapeDtypeStruct((1, hidden // replicas, width), F32)],
        in_specs=[VMEM],
        out_specs=[VMEM] * 3,
        compiler_params=pltpu.CompilerParams(vmem_limit_bytes=8 * 1024 * 1024),
    )(parts)

    b = send(add(b, g_b2, SIDE_FLOPS), home)
    a = send(add(a, g_a3), home)
    b = send(add(b, g_b1, SIDE_FLOPS), uncross)
    a = send(add(a, g_a2), home)
    a = send(add(a, g_a1), home)
    token_grad, gate_grad = pl.pallas_call(
        finish_kernel,
        out_shape=[jax.ShapeDtypeStruct((rows, width), BF), jax.ShapeDtypeStruct(gates.shape[::-1], BF)],
        in_specs=[VMEM] * 4,
        out_specs=[VMEM] * 2,
        compiler_params=pltpu.CompilerParams(vmem_limit_bytes=8 * 1024 * 1024),
    )(routing.T, a, b, g_own)
    return token_grad, gate_grad.T, *sums


def solution(mesh):
    in_specs = (
        P(("dp", "expert"), None),
        P(("dp", "expert"), None),
        P(("dp", "expert"), None),
        P(("dp", "expert"), None),
        P("expert", None, None),
        P("expert", None, None),
        P("expert", None, None),
    )
    out_specs = (
        P(("dp", "expert"), None),
        P(("dp", "expert"), None),
        P("expert", "dp", None),
        P("expert", "dp", None),
        P("expert", "dp", None),
    )
    return jax.shard_map(
        on_device, mesh=mesh, in_specs=in_specs, out_specs=out_specs, check_vma=False
    )
```

```python
import functools
import math

import jax
import jax.numpy as jnp
from jax import lax
from jax.experimental import pallas as pl
from jax.experimental.pallas import tpu as pltpu
from jax.sharding import PartitionSpec as P

BF = jnp.bfloat16
F32 = jnp.float32
LANES = 128
HOP_FLOPS = 5_000_000_000
SIDE_FLOPS = 2_500_000_000


def dot(a, b, ca, cb):
    return lax.dot_general(a, b, (((ca,), (cb,)), ((), ())), preferred_element_type=F32)


def pack_kernel(routing, gates, tokens, cotangent, out, named_ref, gate_ref, sems):
    rows, width = tokens.shape
    small = [pltpu.make_async_copy(routing, named_ref, sems.at[0]), pltpu.make_async_copy(gates, gate_ref, sems.at[1])]
    large = [
        pltpu.make_async_copy(tokens, out.at[:, pl.ds(0, width)], sems.at[2]),
        pltpu.make_async_copy(cotangent, out.at[:, pl.ds(width, width)], sems.at[3]),
    ]
    for copy in small + large:
        copy.start()
    for copy in small:
        copy.wait()
    expert = lax.broadcasted_iota(jnp.int32, (LANES, rows), 0)
    dense = jnp.zeros((LANES, rows), F32)
    named, gate = named_ref[...], gate_ref[...].astype(F32)
    for k in range(routing.shape[0]):
        dense = jnp.where(expert == named[k : k + 1], gate[k : k + 1], dense)
    out[:, 2 * width :] = dense.T.astype(BF)
    for copy in large:
        copy.wait()


def finish_kernel(routing, p, q, r, token_grad, gate_grad):
    rows, width = token_grad.shape
    total = p[...].astype(F32) + q[...].astype(F32) + r[...].astype(F32)
    token_grad[...] = total[:, :width].astype(BF)
    terms = total[:, width:].T
    expert = lax.broadcasted_iota(jnp.int32, (LANES, rows), 0)
    named = routing[...]
    picked = [
        jnp.sum(jnp.where(expert == named[k : k + 1], terms, 0.0), axis=0, keepdims=True)
        for k in range(routing.shape[0])
    ]
    gate_grad[...] = jnp.concatenate(picked, axis=0).astype(BF)


def split(blocks, width):
    x = jnp.concatenate([b[:, :width] for b in blocks], axis=0)
    dy = jnp.concatenate([b[:, width : 2 * width] for b in blocks], axis=0)
    dense = jnp.concatenate([b[:, 2 * width :] for b in blocks], axis=0).astype(F32)
    return x, dy, dense


def one_expert(x, dy, g, w_gate, w_up, w_down):
    pre_gate, pre_up = dot(x, w_gate[...], 1, 0), dot(x, w_up[...], 1, 0)
    back = dot(dy, w_down[...], 1, 1)
    sig = jax.nn.sigmoid(pre_gate)
    silu = pre_gate * sig
    act = silu * pre_up
    act_grad = g * back
    gate_pre = (act_grad * pre_up * sig * (1.0 + pre_gate * (1.0 - sig))).astype(BF)
    up_pre = (act_grad * silu).astype(BF)
    return gate_pre, up_pre, (g * act).astype(BF), jnp.sum(act * back, axis=1, keepdims=True)


def both_experts(blocks, weights, mine, out_grads):
    width = weights[0][0].shape[0]
    x, dy, dense = split(blocks, width)
    lane = lax.broadcasted_iota(jnp.int32, dense.shape, 1)
    terms = jnp.zeros(dense.shape, F32)
    grad = jnp.zeros(x.shape, F32)
    grads, acts = [], []
    for j, (w_gate, w_up, w_down) in enumerate(weights):
        here = lane == (mine if j == 0 else mine + 1 - 2 * lax.rem(mine, 2))
        g = jnp.sum(jnp.where(here, dense, 0.0), axis=1, keepdims=True)
        gate_pre, up_pre, act, term = one_expert(x, dy, g, w_gate, w_up, w_down)
        terms = terms + jnp.where(here, term, 0.0)
        grads += [gate_pre, up_pre]
        acts.append(act)
        grad = grad + dot(gate_pre, w_gate[...], 1, 1) + dot(up_pre, w_up[...], 1, 1)
    rows = blocks[0].shape[0]
    for i, out in enumerate(out_grads):
        out[:, :width] = grad[i * rows : (i + 1) * rows].astype(BF)
        out[:, width:] = terms[i * rows : (i + 1) * rows].astype(BF)
    return x, dy, grads, acts


def put(outs, where, value):
    at = 0
    for out in outs:
        wide = out.shape[-1]
        out[where] = value[..., at : at + wide]
        at += wide


def to_parts(outs, d_gu, first_row):
    nx, _, rows, _ = outs[0].shape
    n = rows * 2 // 3
    y, ys = first_row // (nx * n), d_gu.shape[0] // (nx * n)
    pieces = d_gu.astype(BF).reshape(ys, nx, n, d_gu.shape[1])
    for x in range(nx):
        put(outs, (x, slice(y, y + ys), slice(0, n)), pieces[:, x])


def down_to_parts(outs, d_down, early=()):
    nx, ny, rows, _ = outs[0].shape
    m, half = rows // 3 // 2, d_down.shape[1] // 2
    pieces = [d_down[:, c : c + half].reshape(ny, nx, m, half) for c in (0, half)]
    pieces = jnp.concatenate(pieces, axis=2)
    for x in range(nx):
        piece, where = pieces[:, x], (x, slice(0, ny), slice(rows - 2 * m, rows))
        if early:
            piece = piece + jnp.concatenate([e[where] for e in early], axis=-1).astype(F32)
        put(outs, where, piece.astype(BF))


def group_kernel(first, swap, n_blocks, expert_ref, *refs):
    blocks, refs = refs[:n_blocks], refs[n_blocks:]
    weights, refs = (refs[:3], refs[3:6]), refs[6:]
    if not first:
        (acc_gu, acc_d), refs = refs[:2], refs[2:]
    out_grads, outs = refs[:n_blocks], refs[n_blocks:]
    width, hidden = weights[0][0].shape
    x, dy, grads, acts = both_experts(blocks, weights, expert_ref[0], out_grads)
    grads = jnp.concatenate(grads, axis=1)
    for rows in steps(outs, swap, width, hidden):
        d_gu = dot(x[:, rows], grads, 0, 0)
        if not first:
            d_gu = d_gu + acc_gu[rows, :]
        if swap:
            outs[0][rows, :] = d_gu[:, : 2 * hidden]
            to_parts(outs[2:], d_gu[:, 2 * hidden :], rows.start)
        else:
            outs[0][rows, :] = d_gu
    for j, act in enumerate(acts):
        rows = slice(j * hidden, (j + 1) * hidden)
        d_down = dot(act, dy, 0, 0)
        if not first:
            d_down = d_down + acc_d[rows, :]
        if swap and j == 1:
            down_to_parts(outs[2:], d_down)
        else:
            outs[1][rows, :] = d_down


def steps(outs, swap, width, hidden):
    step = max(width // outs[2].shape[1], 2 * hidden) if swap else 2 * hidden
    return [slice(r, r + step) for r in range(0, width, step)]


def far_kernel(expert_ref, block, *refs):
    weights, (out_grad, out_pre, out_act) = (refs[:3], refs[3:6]), refs[6:]
    _, _, grads, acts = both_experts([block], weights, expert_ref[0], [out_grad])
    out_pre[...] = jnp.concatenate(grads[:2], axis=1)
    out_act[...] = acts[0]


def last_kernel(expert_ref, block, pre, act, theirs, w_gate, w_up, w_down, acc_gu, acc_d, *refs):
    *early, out, made, sems = refs
    width, hidden = w_gate.shape
    x, dy, dense = split([theirs], width)
    here = lax.broadcasted_iota(jnp.int32, dense.shape, 1) == expert_ref[0]
    g = jnp.sum(jnp.where(here, dense, 0.0), axis=1, keepdims=True)
    gate_pre, up_pre, gated, _ = one_expert(x, dy, g, w_gate, w_up, w_down)
    x = jnp.concatenate([block[:, :width], x], axis=0)
    dy = jnp.concatenate([block[:, width : 2 * width], dy], axis=0)
    grads = jnp.concatenate([pre[...], jnp.concatenate([gate_pre, up_pre], axis=1)], axis=0)
    gated = jnp.concatenate([act[...], gated], axis=0)
    nx, ny, rows, wide = out.shape
    n = rows * 2 // 3
    step = max(nx * n, 2 * hidden)
    copies = []

    def leave(*where):
        copies.append(pltpu.make_async_copy(made.at[where], out.at[where], sems.at[len(copies)]))
        copies[-1].start()

    for r in range(0, width, step):
        y, ys = r // (nx * n), step // (nx * n)
        partner = [jnp.stack([e[p, y : y + ys, :n, :] for p in range(nx)], axis=1) for e in early]
        partner = jnp.concatenate(partner, axis=-1)
        d_gu = dot(x[:, r : r + step], grads, 0, 0) + acc_gu[r : r + step, :]
        to_parts([made], d_gu + partner.reshape(step, wide).astype(F32), r)
        leave(slice(None), pl.ds(y, ys), pl.ds(0, n))
    down_to_parts([made], dot(gated, dy, 0, 0) + acc_d[...], early)
    leave(slice(None), slice(None), pl.ds(n, rows - n))
    for copy in copies:
        copy.wait()


def sum_kernel(parts, gate, up, down):
    n, hidden = gate.shape[1:]
    m = down.shape[1]
    total = jnp.sum(parts[...].astype(F32), axis=0)
    gate[0], up[0] = total[:n, :hidden], total[:n, hidden:]
    down[0] = jnp.concatenate([total[n : n + m], total[n + m :]], axis=1)


VMEM = pl.BlockSpec(memory_space=pltpu.VMEM)


def call(kernel, out_shape, expert, operands, aliases, flops, out_specs=VMEM, scratch=()):
    return pl.pallas_call(
        kernel,
        out_shape=out_shape,
        in_specs=[pl.BlockSpec(memory_space=pltpu.SMEM)] + [VMEM] * len(operands),
        out_specs=[out_specs] * len(out_shape),
        scratch_shapes=scratch,
        input_output_aliases=aliases,
        compiler_params=pltpu.CompilerParams(vmem_limit_bytes=26 * 1024 * 1024),
        cost_estimate=pl.CostEstimate(flops=flops, bytes_accessed=16 * 1024 * 1024, transcendentals=0),
    )(expert, *operands)


def group(expert, blocks, weights, acc, replicas=()):
    rows = blocks[0].shape[0]
    width, hidden = weights[0].shape
    own = 2 * hidden if replicas else 4 * hidden
    shapes = [jax.ShapeDtypeStruct((rows, width + LANES), BF)] * len(blocks) + [
        jax.ShapeDtypeStruct((width, own), F32),
        jax.ShapeDtypeStruct((own // 2, width), F32),
    ]
    if replicas:
        shapes += [jax.ShapeDtypeStruct((*replicas, (width + 2 * hidden) // math.prod(replicas), hidden), BF)] * 2
    n = len(blocks)
    return call(
        functools.partial(group_kernel, not acc, bool(replicas), n),
        shapes,
        expert,
        (*blocks, *weights, *acc),
        {7 + n: n, 8 + n: n + 1} if acc and not replicas else {},
        2 * n * rows * width * hidden * 16,
    )


def add_kernel(p, q, out):
    out[...] = (p[...].astype(F32) + q[...].astype(F32)).astype(BF)


def add(p, q, flops=HOP_FLOPS):
    return pl.pallas_call(
        add_kernel,
        out_shape=jax.ShapeDtypeStruct(p.shape, BF),
        in_specs=[VMEM] * 2,
        out_specs=VMEM,
        compiler_params=pltpu.CompilerParams(vmem_limit_bytes=8 * 1024 * 1024),
        cost_estimate=pl.CostEstimate(flops=flops, bytes_accessed=3 * 2 * p.size, transcendentals=0),
    )(p, q)


def after(a, *others):
    return lax.optimization_barrier((a, *others))[0]


def on_device(tokens, cotangent, routing, gates, gate_weight, up_weight, down_weight):
    groups = lax.axis_size("expert")
    replicas = lax.axis_size("dp")
    nx, ny = 1, replicas
    rows, width = tokens.shape
    hidden = gate_weight.shape[2]
    out = [(i, (i + 2 if i % 2 == 0 else i - 2) % groups) for i in range(groups)]
    home = [(b, a) for a, b in out]
    swap = [(i, i ^ 1) for i in range(groups)]
    cross = [(i, (i - 1 if i % 2 == 0 else i + 1) % groups) for i in range(groups)]
    uncross = [(b, a) for a, b in cross]

    def send(a, pairs):
        return lax.ppermute(a, "expert", pairs)

    in_hbm = pl.BlockSpec(memory_space=pltpu.HBM)
    own = pl.pallas_call(
        pack_kernel,
        out_shape=jax.ShapeDtypeStruct((rows, 2 * width + LANES), BF),
        in_specs=[in_hbm] * 4,
        out_specs=VMEM,
        scratch_shapes=[
            pltpu.VMEM(routing.shape[::-1], jnp.int32),
            pltpu.VMEM(gates.shape[::-1], BF),
            pltpu.SemaphoreType.DMA((4,)),
        ],
        compiler_params=pltpu.CompilerParams(vmem_limit_bytes=58 * 1024 * 1024),
    )(routing.T, gates.T, tokens, cotangent)
    expert = lax.axis_index("expert").astype(jnp.int32).reshape(1)

    a1 = send(own, out)
    b1 = send(own, cross)
    weights = [gate_weight[0], up_weight[0], down_weight[0]]
    weights = weights + [send(w, swap) for w in weights]
    a2 = send(a1, out)
    g_own, g_a1, *acc = group(expert, (own, a1), weights, ())
    b2 = send(b1, out)
    a3 = send(after(a2, g_a1), out)
    g_b1, g_a2, *acc = group(expert, (b1, a2), weights, acc)
    b3 = send(b2, out)
    a4 = send(after(a3, g_a2), out)
    g_b2, g_a3, *acc = group(expert, (b2, a3), weights, acc)
    g_b3, *acc, early0, early1 = group(expert, (b3,), weights, acc, (nx, ny))
    early = [send(early0, swap), send(early1, swap)]
    whole = jax.ShapeDtypeStruct((*early0.shape[:-1], 2 * hidden), BF)
    theirs = send(a4, swap)
    g_a4, pre, act = call(
        far_kernel,
        [
            jax.ShapeDtypeStruct((rows, width + LANES), BF),
            jax.ShapeDtypeStruct((rows, 2 * hidden), BF),
            jax.ShapeDtypeStruct((rows, hidden), BF),
        ],
        expert,
        (a4, *weights),
        {},
        2 * rows * width * hidden * 10,
    )
    (parts,) = call(
        last_kernel,
        [whole],
        expert,
        (a4, pre, act, theirs, *weights[:3], *acc, *early),
        {},
        2 * rows * width * hidden * 9,
        in_hbm,
        [pltpu.VMEM(whole.shape, BF), pltpu.SemaphoreType.DMA((8,))],
    )

    b = send(g_b3, home)
    a = send(g_a4, home)

    parts = lax.all_to_all(parts[0], "dp", split_axis=0, concat_axis=0, tiled=True)
    slab = jax.ShapeDtypeStruct((1, width // replicas, hidden), F32)
    sums = pl.pallas_call(
        sum_kernel,
        out_shape=[slab, slab, jax.ShapeDtypeStruct((1, hidden // replicas, width), F32)],
        in_specs=[VMEM],
        out_specs=[VMEM] * 3,
        compiler_params=pltpu.CompilerParams(vmem_limit_bytes=8 * 1024 * 1024),
    )(parts)

    b = send(add(b, g_b2, SIDE_FLOPS), home)
    a = send(add(a, g_a3), home)
    b = send(add(b, g_b1, SIDE_FLOPS), uncross)
    a = send(add(a, g_a2), home)
    a = send(add(a, g_a1), home)
    token_grad, gate_grad = pl.pallas_call(
        finish_kernel,
        out_shape=[jax.ShapeDtypeStruct((rows, width), BF), jax.ShapeDtypeStruct(gates.shape[::-1], BF)],
        in_specs=[VMEM] * 4,
        out_specs=[VMEM] * 2,
        compiler_params=pltpu.CompilerParams(vmem_limit_bytes=8 * 1024 * 1024),
    )(routing.T, a, b, g_own)
    return token_grad, gate_grad.T, *sums


def solution(mesh):
    in_specs = (
        P(("dp", "expert"), None),
        P(("dp", "expert"), None),
        P(("dp", "expert"), None),
        P(("dp", "expert"), None),
        P("expert", None, None),
        P("expert", None, None),
        P("expert", None, None),
    )
    out_specs = (
        P(("dp", "expert"), None),
        P(("dp", "expert"), None),
        P("expert", "dp", None),
        P("expert", "dp", None),
        P("expert", "dp", None),
    )
    return jax.shard_map(
        on_device, mesh=mesh, in_specs=in_specs, out_specs=out_specs, check_vma=False
    )
```

```python
import functools
import math

import jax
import jax.numpy as jnp
from jax import lax
from jax.experimental import pallas as pl
from jax.experimental.pallas import tpu as pltpu
from jax.sharding import PartitionSpec as P

BF = jnp.bfloat16
F32 = jnp.float32
LANES = 128
HOP_FLOPS = 3_000_000_000
SIDE_FLOPS = 500_000_000


def dot(a, b, ca, cb):
    return lax.dot_general(a, b, (((ca,), (cb,)), ((), ())), preferred_element_type=F32)


def pack_kernel(routing, gates, tokens, cotangent, out, named_ref, gate_ref, sems):
    rows, width = tokens.shape
    small = [pltpu.make_async_copy(routing, named_ref, sems.at[0]), pltpu.make_async_copy(gates, gate_ref, sems.at[1])]
    large = [
        pltpu.make_async_copy(tokens, out.at[:, pl.ds(0, width)], sems.at[2]),
        pltpu.make_async_copy(cotangent, out.at[:, pl.ds(width, width)], sems.at[3]),
    ]
    for copy in small + large:
        copy.start()
    for copy in small:
        copy.wait()
    expert = lax.broadcasted_iota(jnp.int32, (LANES, rows), 0)
    dense = jnp.zeros((LANES, rows), F32)
    named, gate = named_ref[...], gate_ref[...].astype(F32)
    for k in range(routing.shape[0]):
        dense = jnp.where(expert == named[k : k + 1], gate[k : k + 1], dense)
    out[:, 2 * width :] = dense.T.astype(BF)
    for copy in large:
        copy.wait()


def finish_kernel(routing, p, q, r, token_grad, gate_grad):
    rows, width = token_grad.shape
    total = p[...].astype(F32) + q[...].astype(F32) + r[...].astype(F32)
    token_grad[...] = total[:, :width].astype(BF)
    terms = total[:, width:].T
    expert = lax.broadcasted_iota(jnp.int32, (LANES, rows), 0)
    named = routing[...]
    picked = [
        jnp.sum(jnp.where(expert == named[k : k + 1], terms, 0.0), axis=0, keepdims=True)
        for k in range(routing.shape[0])
    ]
    gate_grad[...] = jnp.concatenate(picked, axis=0).astype(BF)


def split(blocks, width):
    x = jnp.concatenate([b[:, :width] for b in blocks], axis=0)
    dy = jnp.concatenate([b[:, width : 2 * width] for b in blocks], axis=0)
    dense = jnp.concatenate([b[:, 2 * width :] for b in blocks], axis=0).astype(F32)
    return x, dy, dense


def one_expert(x, dy, g, w_gate, w_up, w_down):
    pre_gate, pre_up = dot(x, w_gate[...], 1, 0), dot(x, w_up[...], 1, 0)
    back = dot(dy, w_down[...], 1, 1)
    sig = jax.nn.sigmoid(pre_gate)
    silu = pre_gate * sig
    act = silu * pre_up
    act_grad = g * back
    gate_pre = (act_grad * pre_up * sig * (1.0 + pre_gate * (1.0 - sig))).astype(BF)
    up_pre = (act_grad * silu).astype(BF)
    return gate_pre, up_pre, (g * act).astype(BF), jnp.sum(act * back, axis=1, keepdims=True)


def both_experts(blocks, weights, mine, out_grads):
    width = weights[0][0].shape[0]
    x, dy, dense = split(blocks, width)
    lane = lax.broadcasted_iota(jnp.int32, dense.shape, 1)
    terms = jnp.zeros(dense.shape, F32)
    grad = jnp.zeros(x.shape, F32)
    grads, acts = [], []
    for j, (w_gate, w_up, w_down) in enumerate(weights):
        here = lane == (mine if j == 0 else mine + 1 - 2 * lax.rem(mine, 2))
        g = jnp.sum(jnp.where(here, dense, 0.0), axis=1, keepdims=True)
        gate_pre, up_pre, act, term = one_expert(x, dy, g, w_gate, w_up, w_down)
        terms = terms + jnp.where(here, term, 0.0)
        grads += [gate_pre, up_pre]
        acts.append(act)
        grad = grad + dot(gate_pre, w_gate[...], 1, 1) + dot(up_pre, w_up[...], 1, 1)
    rows = blocks[0].shape[0]
    for i, out in enumerate(out_grads):
        out[:, :width] = grad[i * rows : (i + 1) * rows].astype(BF)
        out[:, width:] = terms[i * rows : (i + 1) * rows].astype(BF)
    return x, dy, grads, acts


def put(outs, where, value):
    at = 0
    for out in outs:
        wide = out.shape[-1]
        out[where] = value[..., at : at + wide]
        at += wide


def to_parts(outs, d_gu, first_row):
    nx, _, rows, _ = outs[0].shape
    n = rows * 2 // 3
    y, ys = first_row // (nx * n), d_gu.shape[0] // (nx * n)
    pieces = d_gu.astype(BF).reshape(ys, nx, n, d_gu.shape[1])
    for x in range(nx):
        put(outs, (x, slice(y, y + ys), slice(0, n)), pieces[:, x])


def down_to_parts(outs, d_down, early=()):
    nx, ny, rows, _ = outs[0].shape
    m, half = rows // 3 // 2, d_down.shape[1] // 2
    pieces = [d_down[:, c : c + half].reshape(ny, nx, m, half) for c in (0, half)]
    pieces = jnp.concatenate(pieces, axis=2)
    for x in range(nx):
        piece, where = pieces[:, x], (x, slice(0, ny), slice(rows - 2 * m, rows))
        if early:
            piece = piece + jnp.concatenate([e[where] for e in early], axis=-1).astype(F32)
        put(outs, where, piece.astype(BF))


def group_kernel(first, swap, n_blocks, expert_ref, *refs):
    blocks, refs = refs[:n_blocks], refs[n_blocks:]
    weights, refs = (refs[:3], refs[3:6]), refs[6:]
    if not first:
        (acc_gu, acc_d), refs = refs[:2], refs[2:]
    out_grads, outs = refs[:n_blocks], refs[n_blocks:]
    width, hidden = weights[0][0].shape
    x, dy, grads, acts = both_experts(blocks, weights, expert_ref[0], out_grads)
    grads = jnp.concatenate(grads, axis=1)
    for rows in steps(outs, swap, width, hidden):
        d_gu = dot(x[:, rows], grads, 0, 0)
        if not first:
            d_gu = d_gu + acc_gu[rows, :]
        if swap:
            outs[0][rows, :] = d_gu[:, : 2 * hidden]
            to_parts(outs[2:], d_gu[:, 2 * hidden :], rows.start)
        else:
            outs[0][rows, :] = d_gu
    for j, act in enumerate(acts):
        rows = slice(j * hidden, (j + 1) * hidden)
        d_down = dot(act, dy, 0, 0)
        if not first:
            d_down = d_down + acc_d[rows, :]
        if swap and j == 1:
            down_to_parts(outs[2:], d_down)
        else:
            outs[1][rows, :] = d_down


def steps(outs, swap, width, hidden):
    step = max(width // outs[2].shape[1], 2 * hidden) if swap else 2 * hidden
    return [slice(r, r + step) for r in range(0, width, step)]


def far_kernel(expert_ref, block, *refs):
    weights, (out_grad, out_pre, out_act) = (refs[:3], refs[3:6]), refs[6:]
    _, _, grads, acts = both_experts([block], weights, expert_ref[0], [out_grad])
    out_pre[...] = jnp.concatenate(grads[:2], axis=1)
    out_act[...] = acts[0]


def last_kernel(expert_ref, block, pre, act, theirs, w_gate, w_up, w_down, acc_gu, acc_d, *refs):
    *early, out, made, sems = refs
    width, hidden = w_gate.shape
    x, dy, dense = split([theirs], width)
    here = lax.broadcasted_iota(jnp.int32, dense.shape, 1) == expert_ref[0]
    g = jnp.sum(jnp.where(here, dense, 0.0), axis=1, keepdims=True)
    gate_pre, up_pre, gated, _ = one_expert(x, dy, g, w_gate, w_up, w_down)
    x = jnp.concatenate([block[:, :width], x], axis=0)
    dy = jnp.concatenate([block[:, width : 2 * width], dy], axis=0)
    grads = jnp.concatenate([pre[...], jnp.concatenate([gate_pre, up_pre], axis=1)], axis=0)
    gated = jnp.concatenate([act[...], gated], axis=0)
    nx, ny, rows, wide = out.shape
    n = rows * 2 // 3
    step = max(nx * n, 2 * hidden)
    copies = []

    def leave(*where):
        copies.append(pltpu.make_async_copy(made.at[where], out.at[where], sems.at[len(copies)]))
        copies[-1].start()

    for r in range(0, width, step):
        y, ys = r // (nx * n), step // (nx * n)
        partner = [jnp.stack([e[p, y : y + ys, :n, :] for p in range(nx)], axis=1) for e in early]
        partner = jnp.concatenate(partner, axis=-1)
        d_gu = dot(x[:, r : r + step], grads, 0, 0) + acc_gu[r : r + step, :]
        to_parts([made], d_gu + partner.reshape(step, wide).astype(F32), r)
        leave(slice(None), pl.ds(y, ys), pl.ds(0, n))
    down_to_parts([made], dot(gated, dy, 0, 0) + acc_d[...], early)
    leave(slice(None), slice(None), pl.ds(n, rows - n))
    for copy in copies:
        copy.wait()


def halfway_kernel(parts, out):
    out[...] = jnp.sum(parts[...].astype(F32), axis=0).astype(BF)


def sum_kernel(parts, gate, up, down):
    n, hidden = gate.shape[1:]
    m = down.shape[1]
    total = jnp.sum(parts[...].astype(F32), axis=0)
    gate[0], up[0] = total[:n, :hidden], total[:n, hidden:]
    down[0] = jnp.concatenate([total[n : n + m], total[n + m :]], axis=1)


VMEM = pl.BlockSpec(memory_space=pltpu.VMEM)


def call(kernel, out_shape, expert, operands, aliases, flops, out_specs=VMEM, scratch=()):
    return pl.pallas_call(
        kernel,
        out_shape=out_shape,
        in_specs=[pl.BlockSpec(memory_space=pltpu.SMEM)] + [VMEM] * len(operands),
        out_specs=[out_specs] * len(out_shape),
        scratch_shapes=scratch,
        input_output_aliases=aliases,
        compiler_params=pltpu.CompilerParams(vmem_limit_bytes=26 * 1024 * 1024),
        cost_estimate=pl.CostEstimate(flops=flops, bytes_accessed=16 * 1024 * 1024, transcendentals=0),
    )(expert, *operands)


def group(expert, blocks, weights, acc, replicas=()):
    rows = blocks[0].shape[0]
    width, hidden = weights[0].shape
    own = 2 * hidden if replicas else 4 * hidden
    shapes = [jax.ShapeDtypeStruct((rows, width + LANES), BF)] * len(blocks) + [
        jax.ShapeDtypeStruct((width, own), F32),
        jax.ShapeDtypeStruct((own // 2, width), F32),
    ]
    if replicas:
        shapes += [jax.ShapeDtypeStruct((*replicas, (width + 2 * hidden) // math.prod(replicas), hidden), BF)] * 2
    n = len(blocks)
    return call(
        functools.partial(group_kernel, not acc, bool(replicas), n),
        shapes,
        expert,
        (*blocks, *weights, *acc),
        {7 + n: n, 8 + n: n + 1} if acc and not replicas else {},
        2 * n * rows * width * hidden * 16,
    )


def add_kernel(p, q, out):
    out[...] = (p[...].astype(F32) + q[...].astype(F32)).astype(BF)


def add(p, q, flops=HOP_FLOPS):
    return pl.pallas_call(
        add_kernel,
        out_shape=jax.ShapeDtypeStruct(p.shape, BF),
        in_specs=[VMEM] * 2,
        out_specs=VMEM,
        compiler_params=pltpu.CompilerParams(vmem_limit_bytes=8 * 1024 * 1024),
        cost_estimate=pl.CostEstimate(flops=flops, bytes_accessed=3 * 2 * p.size, transcendentals=0),
    )(p, q)


def after(a, *others):
    return lax.optimization_barrier((a, *others))[0]


def on_device(tokens, cotangent, routing, gates, gate_weight, up_weight, down_weight):
    groups = lax.axis_size("expert")
    replicas = lax.axis_size("dp")
    nx = 4 if replicas % 4 == 0 else 1
    ny = replicas // nx
    along_x = [[y * nx + x for x in range(nx)] for y in range(ny)]
    along_y = [[y * nx + x for y in range(ny)] for x in range(nx)]
    rows, width = tokens.shape
    hidden = gate_weight.shape[2]
    out = [(i, (i + 2 if i % 2 == 0 else i - 2) % groups) for i in range(groups)]
    home = [(b, a) for a, b in out]
    swap = [(i, i ^ 1) for i in range(groups)]
    cross = [(i, (i - 1 if i % 2 == 0 else i + 1) % groups) for i in range(groups)]
    uncross = [(b, a) for a, b in cross]

    def send(a, pairs):
        return lax.ppermute(a, "expert", pairs)

    in_hbm = pl.BlockSpec(memory_space=pltpu.HBM)
    own = pl.pallas_call(
        pack_kernel,
        out_shape=jax.ShapeDtypeStruct((rows, 2 * width + LANES), BF),
        in_specs=[in_hbm] * 4,
        out_specs=VMEM,
        scratch_shapes=[
            pltpu.VMEM(routing.shape[::-1], jnp.int32),
            pltpu.VMEM(gates.shape[::-1], BF),
            pltpu.SemaphoreType.DMA((4,)),
        ],
        compiler_params=pltpu.CompilerParams(vmem_limit_bytes=58 * 1024 * 1024),
    )(routing.T, gates.T, tokens, cotangent)
    expert = lax.axis_index("expert").astype(jnp.int32).reshape(1)

    a1 = send(own, out)
    b1 = send(own, cross)
    weights = [gate_weight[0], up_weight[0], down_weight[0]]
    weights = weights + [send(w, swap) for w in weights]
    a2 = send(a1, out)
    g_own, g_a1, *acc = group(expert, (own, a1), weights, ())
    b2 = send(b1, out)
    a3 = send(after(a2, g_a1), out)
    g_b1, g_a2, *acc = group(expert, (b1, a2), weights, acc)
    b3 = send(b2, out)
    a4 = send(after(a3, g_a2), out)
    g_b2, g_a3, *acc = group(expert, (b2, a3), weights, acc)
    g_b3, *acc, early0, early1 = group(expert, (b3,), weights, acc, (nx, ny))
    early = [send(early0, swap), send(early1, swap)]
    whole = jax.ShapeDtypeStruct((*early0.shape[:-1], 2 * hidden), BF)
    theirs = send(a4, swap)
    g_a4, pre, act = call(
        far_kernel,
        [
            jax.ShapeDtypeStruct((rows, width + LANES), BF),
            jax.ShapeDtypeStruct((rows, 2 * hidden), BF),
            jax.ShapeDtypeStruct((rows, hidden), BF),
        ],
        expert,
        (a4, *weights),
        {},
        2 * rows * width * hidden * 10,
    )
    (parts,) = call(
        last_kernel,
        [whole],
        expert,
        (a4, pre, act, theirs, *weights[:3], *acc, *early),
        {},
        2 * rows * width * hidden * 9,
        in_hbm,
        [pltpu.VMEM(whole.shape, BF), pltpu.SemaphoreType.DMA((8,))],
    )

    b = send(g_b3, home)
    a = send(g_a4, home)

    if nx > 1:
        parts = lax.all_to_all(parts, "dp", split_axis=0, concat_axis=0, axis_index_groups=along_x, tiled=True)
    parts = pl.pallas_call(
        halfway_kernel,
        out_shape=jax.ShapeDtypeStruct(parts.shape[1:], BF),
        in_specs=[VMEM],
        out_specs=VMEM,
        compiler_params=pltpu.CompilerParams(vmem_limit_bytes=8 * 1024 * 1024),
    )(parts)
    if ny > 1:
        parts = lax.all_to_all(parts, "dp", split_axis=0, concat_axis=0, axis_index_groups=along_y, tiled=True)
    slab = jax.ShapeDtypeStruct((1, width // replicas, hidden), F32)
    sums = pl.pallas_call(
        sum_kernel,
        out_shape=[slab, slab, jax.ShapeDtypeStruct((1, hidden // replicas, width), F32)],
        in_specs=[VMEM],
        out_specs=[VMEM] * 3,
        compiler_params=pltpu.CompilerParams(vmem_limit_bytes=8 * 1024 * 1024),
    )(parts)

    b = send(add(b, g_b2, SIDE_FLOPS), home)
    a = send(add(a, g_a3, SIDE_FLOPS), home)
    b = send(add(b, g_b1, SIDE_FLOPS), uncross)
    a = send(add(a, g_a2), home)
    a = send(add(a, g_a1), home)
    token_grad, gate_grad = pl.pallas_call(
        finish_kernel,
        out_shape=[jax.ShapeDtypeStruct((rows, width), BF), jax.ShapeDtypeStruct(gates.shape[::-1], BF)],
        in_specs=[VMEM] * 4,
        out_specs=[VMEM] * 2,
        compiler_params=pltpu.CompilerParams(vmem_limit_bytes=8 * 1024 * 1024),
    )(routing.T, a, b, g_own)
    return token_grad, gate_grad.T, *sums


def solution(mesh):
    in_specs = (
        P(("dp", "expert"), None),
        P(("dp", "expert"), None),
        P(("dp", "expert"), None),
        P(("dp", "expert"), None),
        P("expert", None, None),
        P("expert", None, None),
        P("expert", None, None),
    )
    out_specs = (
        P(("dp", "expert"), None),
        P(("dp", "expert"), None),
        P("expert", "dp", None),
        P("expert", "dp", None),
        P("expert", "dp", None),
    )
    return jax.shard_map(
        on_device, mesh=mesh, in_specs=in_specs, out_specs=out_specs, check_vma=False
    )
```

```python
import functools
import math

import jax
import jax.numpy as jnp
from jax import lax
from jax.experimental import pallas as pl
from jax.experimental.pallas import tpu as pltpu
from jax.sharding import PartitionSpec as P

BF = jnp.bfloat16
F32 = jnp.float32
LANES = 128
HOP_FLOPS = 5_000_000_000
SIDE_FLOPS = 2_500_000_000
FAR_FLOPS = 15_000_000_000


def dot(a, b, ca, cb):
    return lax.dot_general(a, b, (((ca,), (cb,)), ((), ())), preferred_element_type=F32)


def pack_kernel(routing, gates, tokens, cotangent, out, named_ref, gate_ref, sems):
    rows, width = tokens.shape
    small = [pltpu.make_async_copy(routing, named_ref, sems.at[0]), pltpu.make_async_copy(gates, gate_ref, sems.at[1])]
    large = [
        pltpu.make_async_copy(tokens, out.at[:, pl.ds(0, width)], sems.at[2]),
        pltpu.make_async_copy(cotangent, out.at[:, pl.ds(width, width)], sems.at[3]),
    ]
    for copy in small + large:
        copy.start()
    for copy in small:
        copy.wait()
    expert = lax.broadcasted_iota(jnp.int32, (LANES, rows), 0)
    dense = jnp.zeros((LANES, rows), F32)
    named, gate = named_ref[...], gate_ref[...].astype(F32)
    for k in range(routing.shape[0]):
        dense = jnp.where(expert == named[k : k + 1], gate[k : k + 1], dense)
    out[:, 2 * width :] = dense.T.astype(BF)
    for copy in large:
        copy.wait()


def finish_kernel(parts, routing, p, q, r, token_grad, gate_grad, gate, up, down):
    rows, width = token_grad.shape
    total = p[...].astype(F32) + q[...].astype(F32) + r[...].astype(F32)
    token_grad[...] = total[:, :width].astype(BF)
    terms = total[:, width:].T
    expert = lax.broadcasted_iota(jnp.int32, (LANES, rows), 0)
    named = routing[...]
    picked = [
        jnp.sum(jnp.where(expert == named[k : k + 1], terms, 0.0), axis=0, keepdims=True)
        for k in range(routing.shape[0])
    ]
    gate_grad[...] = jnp.concatenate(picked, axis=0).astype(BF)
    n, hidden = gate.shape[1:]
    m = down.shape[1]
    total = jnp.sum(parts[...].astype(F32), axis=0)
    gate[0], up[0] = total[:n, :hidden], total[:n, hidden:]
    down[0] = jnp.concatenate([total[n : n + m], total[n + m :]], axis=1)


def split(blocks, width):
    x = jnp.concatenate([b[:, :width] for b in blocks], axis=0)
    dy = jnp.concatenate([b[:, width : 2 * width] for b in blocks], axis=0)
    dense = jnp.concatenate([b[:, 2 * width :] for b in blocks], axis=0).astype(F32)
    return x, dy, dense


def one_expert(x, dy, g, w_gate, w_up, w_down):
    pre_gate, pre_up = dot(x, w_gate[...], 1, 0), dot(x, w_up[...], 1, 0)
    back = dot(dy, w_down[...], 1, 1)
    sig = jax.nn.sigmoid(pre_gate)
    silu = pre_gate * sig
    act = silu * pre_up
    act_grad = g * back
    gate_pre = (act_grad * pre_up * sig * (1.0 + pre_gate * (1.0 - sig))).astype(BF)
    up_pre = (act_grad * silu).astype(BF)
    return gate_pre, up_pre, (g * act).astype(BF), jnp.sum(act * back, axis=1, keepdims=True)


def both_experts(blocks, weights, mine, out_grads):
    width = weights[0][0].shape[0]
    x, dy, dense = split(blocks, width)
    lane = lax.broadcasted_iota(jnp.int32, dense.shape, 1)
    terms = jnp.zeros(dense.shape, F32)
    grad = jnp.zeros(x.shape, F32)
    grads, acts = [], []
    for j, (w_gate, w_up, w_down) in enumerate(weights):
        here = lane == (mine if j == 0 else mine + 1 - 2 * lax.rem(mine, 2))
        g = jnp.sum(jnp.where(here, dense, 0.0), axis=1, keepdims=True)
        gate_pre, up_pre, act, term = one_expert(x, dy, g, w_gate, w_up, w_down)
        terms = terms + jnp.where(here, term, 0.0)
        grads += [gate_pre, up_pre]
        acts.append(act)
        grad = grad + dot(gate_pre, w_gate[...], 1, 1) + dot(up_pre, w_up[...], 1, 1)
    rows = blocks[0].shape[0]
    for i, out in enumerate(out_grads):
        out[:, :width] = grad[i * rows : (i + 1) * rows].astype(BF)
        out[:, width:] = terms[i * rows : (i + 1) * rows].astype(BF)
    return x, dy, grads, acts


def put(outs, where, value):
    at = 0
    for out in outs:
        wide = out.shape[-1]
        out[where] = value[..., at : at + wide]
        at += wide


def to_parts(outs, d_gu, first_row):
    nx, _, rows, _ = outs[0].shape
    n = rows * 2 // 3
    y, ys = first_row // (nx * n), d_gu.shape[0] // (nx * n)
    pieces = d_gu.astype(BF).reshape(ys, nx, n, d_gu.shape[1])
    for x in range(nx):
        put(outs, (x, slice(y, y + ys), slice(0, n)), pieces[:, x])


def down_to_parts(outs, d_down, early=()):
    nx, ny, rows, _ = outs[0].shape
    m, half = rows // 3 // 2, d_down.shape[1] // 2
    pieces = [d_down[:, c : c + half].reshape(ny, nx, m, half) for c in (0, half)]
    pieces = jnp.concatenate(pieces, axis=2)
    for x in range(nx):
        piece, where = pieces[:, x], (x, slice(0, ny), slice(rows - 2 * m, rows))
        if early:
            piece = piece + jnp.concatenate([e[where] for e in early], axis=-1).astype(F32)
        put(outs, where, piece.astype(BF))


def group_kernel(first, swap, n_blocks, expert_ref, *refs):
    blocks, refs = refs[:n_blocks], refs[n_blocks:]
    weights, refs = (refs[:3], refs[3:6]), refs[6:]
    if not first:
        (acc_gu, acc_d), refs = refs[:2], refs[2:]
    out_grads, outs = refs[:n_blocks], refs[n_blocks:]
    width, hidden = weights[0][0].shape
    x, dy, grads, acts = both_experts(blocks, weights, expert_ref[0], out_grads)
    grads = jnp.concatenate(grads, axis=1)
    for rows in steps(outs, swap, width, hidden):
        d_gu = dot(x[:, rows], grads, 0, 0)
        if not first:
            d_gu = d_gu + acc_gu[rows, :]
        if swap:
            outs[0][rows, :] = d_gu[:, : 2 * hidden]
            to_parts(outs[2:], d_gu[:, 2 * hidden :], rows.start)
        else:
            outs[0][rows, :] = d_gu
    for j, act in enumerate(acts):
        rows = slice(j * hidden, (j + 1) * hidden)
        d_down = dot(act, dy, 0, 0)
        if not first:
            d_down = d_down + acc_d[rows, :]
        if swap and j == 1:
            down_to_parts(outs[2:], d_down)
        else:
            outs[1][rows, :] = d_down


def steps(outs, swap, width, hidden):
    step = max(width // outs[2].shape[1], 2 * hidden) if swap else 2 * hidden
    return [slice(r, r + step) for r in range(0, width, step)]


def far_kernel(expert_ref, block, *refs):
    weights, (out_grad, out_pre, out_act) = (refs[:3], refs[3:6]), refs[6:]
    _, _, grads, acts = both_experts([block], weights, expert_ref[0], [out_grad])
    out_pre[...] = jnp.concatenate(grads[:2], axis=1)
    out_act[...] = acts[0]


def last_kernel(expert_ref, block, pre, act, theirs, w_gate, w_up, w_down, acc_gu, acc_d, *refs):
    *early, out, made, sems = refs
    width, hidden = w_gate.shape
    x, dy, dense = split([theirs], width)
    here = lax.broadcasted_iota(jnp.int32, dense.shape, 1) == expert_ref[0]
    g = jnp.sum(jnp.where(here, dense, 0.0), axis=1, keepdims=True)
    gate_pre, up_pre, gated, _ = one_expert(x, dy, g, w_gate, w_up, w_down)
    x = jnp.concatenate([block[:, :width], x], axis=0)
    dy = jnp.concatenate([block[:, width : 2 * width], dy], axis=0)
    grads = jnp.concatenate([pre[...], jnp.concatenate([gate_pre, up_pre], axis=1)], axis=0)
    gated = jnp.concatenate([act[...], gated], axis=0)
    nx, ny, rows, wide = out.shape
    n = rows * 2 // 3
    step = max(nx * n, 2 * hidden)
    copies = []

    def leave(*where):
        copies.append(pltpu.make_async_copy(made.at[where], out.at[where], sems.at[len(copies)]))
        copies[-1].start()

    for r in range(0, width, step):
        y, ys = r // (nx * n), step // (nx * n)
        partner = [jnp.stack([e[p, y : y + ys, :n, :] for p in range(nx)], axis=1) for e in early]
        partner = jnp.concatenate(partner, axis=-1)
        d_gu = dot(x[:, r : r + step], grads, 0, 0) + acc_gu[r : r + step, :]
        to_parts([made], d_gu + partner.reshape(step, wide).astype(F32), r)
        leave(slice(None), pl.ds(y, ys), pl.ds(0, n))
    down_to_parts([made], dot(gated, dy, 0, 0) + acc_d[...], early)
    leave(slice(None), slice(None), pl.ds(n, rows - n))
    for copy in copies:
        copy.wait()


VMEM = pl.BlockSpec(memory_space=pltpu.VMEM)


def call(kernel, out_shape, expert, operands, aliases, flops, out_specs=VMEM, scratch=()):
    return pl.pallas_call(
        kernel,
        out_shape=out_shape,
        in_specs=[pl.BlockSpec(memory_space=pltpu.SMEM)] + [VMEM] * len(operands),
        out_specs=[out_specs] * len(out_shape),
        scratch_shapes=scratch,
        input_output_aliases=aliases,
        compiler_params=pltpu.CompilerParams(vmem_limit_bytes=26 * 1024 * 1024),
        cost_estimate=pl.CostEstimate(flops=flops, bytes_accessed=16 * 1024 * 1024, transcendentals=0),
    )(expert, *operands)


def group(expert, blocks, weights, acc, replicas=()):
    rows = blocks[0].shape[0]
    width, hidden = weights[0].shape
    own = 2 * hidden if replicas else 4 * hidden
    shapes = [jax.ShapeDtypeStruct((rows, width + LANES), BF)] * len(blocks) + [
        jax.ShapeDtypeStruct((width, own), F32),
        jax.ShapeDtypeStruct((own // 2, width), F32),
    ]
    if replicas:
        shapes += [jax.ShapeDtypeStruct((*replicas, (width + 2 * hidden) // math.prod(replicas), 2 * hidden), BF)]
    n = len(blocks)
    return call(
        functools.partial(group_kernel, not acc, bool(replicas), n),
        shapes,
        expert,
        (*blocks, *weights, *acc),
        {7 + n: n, 8 + n: n + 1} if acc and not replicas else {},
        2 * n * rows * width * hidden * 16,
    )


def add_kernel(p, q, out):
    out[...] = (p[...].astype(F32) + q[...].astype(F32)).astype(BF)


def add(p, q, flops=HOP_FLOPS):
    return pl.pallas_call(
        add_kernel,
        out_shape=jax.ShapeDtypeStruct(p.shape, BF),
        in_specs=[VMEM] * 2,
        out_specs=VMEM,
        compiler_params=pltpu.CompilerParams(vmem_limit_bytes=8 * 1024 * 1024),
        cost_estimate=pl.CostEstimate(flops=flops, bytes_accessed=3 * 2 * p.size, transcendentals=0),
    )(p, q)


def after(a, *others):
    return lax.optimization_barrier((a, *others))[0]


def on_device(tokens, cotangent, routing, gates, gate_weight, up_weight, down_weight):
    groups = lax.axis_size("expert")
    replicas = lax.axis_size("dp")
    nx, ny = 1, replicas
    rows, width = tokens.shape
    hidden = gate_weight.shape[2]
    out = [(i, (i + 2 if i % 2 == 0 else i - 2) % groups) for i in range(groups)]
    home = [(b, a) for a, b in out]
    swap = [(i, i ^ 1) for i in range(groups)]
    cross = [(i, (i - 1 if i % 2 == 0 else i + 1) % groups) for i in range(groups)]
    uncross = [(b, a) for a, b in cross]

    def send(a, pairs):
        return lax.ppermute(a, "expert", pairs)

    in_hbm = pl.BlockSpec(memory_space=pltpu.HBM)
    own = pl.pallas_call(
        pack_kernel,
        out_shape=jax.ShapeDtypeStruct((rows, 2 * width + LANES), BF),
        in_specs=[in_hbm] * 4,
        out_specs=VMEM,
        scratch_shapes=[
            pltpu.VMEM(routing.shape[::-1], jnp.int32),
            pltpu.VMEM(gates.shape[::-1], BF),
            pltpu.SemaphoreType.DMA((4,)),
        ],
        compiler_params=pltpu.CompilerParams(vmem_limit_bytes=58 * 1024 * 1024),
    )(routing.T, gates.T, tokens, cotangent)
    expert = lax.axis_index("expert").astype(jnp.int32).reshape(1)

    a1 = send(own, out)
    b1 = send(own, cross)
    weights = [gate_weight[0], up_weight[0], down_weight[0]]
    weights = weights + [send(w, swap) for w in weights]
    a2 = send(a1, out)
    g_own, g_a1, *acc = group(expert, (own, a1), weights, ())
    b2 = send(b1, out)
    a3 = send(after(a2, g_a1), out)
    g_b1, g_a2, *acc = group(expert, (b1, a2), weights, acc)
    b3 = send(b2, out)
    a4 = send(after(a3, g_a2), out)
    g_b2, g_a3, *acc = group(expert, (b2, a3), weights, acc)
    g_b3, *acc, early = group(expert, (b3,), weights, acc, (nx, ny))
    early = send(early, swap)
    whole = jax.ShapeDtypeStruct(early.shape, BF)
    theirs = send(a4, swap)
    g_a4, pre, act = call(
        far_kernel,
        [
            jax.ShapeDtypeStruct((rows, width + LANES), BF),
            jax.ShapeDtypeStruct((rows, 2 * hidden), BF),
            jax.ShapeDtypeStruct((rows, hidden), BF),
        ],
        expert,
        (a4, *weights),
        {},
        FAR_FLOPS,
    )
    (parts,) = call(
        last_kernel,
        [whole],
        expert,
        (a4, pre, act, theirs, *weights[:3], *acc, early),
        {},
        2 * rows * width * hidden * 9,
        in_hbm,
        [pltpu.VMEM(whole.shape, BF), pltpu.SemaphoreType.DMA((8,))],
    )

    b = send(g_b3, home)
    a = send(g_a4, home)

    parts = lax.all_to_all(parts[0], "dp", split_axis=0, concat_axis=0, tiled=True)
    b = send(add(b, g_b2, SIDE_FLOPS), home)
    a = send(add(a, g_a3), home)
    b = send(add(b, g_b1, SIDE_FLOPS), uncross)
    a = send(add(a, g_a2), home)
    a = send(add(a, g_a1), home)
    slab = jax.ShapeDtypeStruct((1, width // replicas, hidden), F32)
    token_grad, gate_grad, *sums = pl.pallas_call(
        finish_kernel,
        out_shape=[
            jax.ShapeDtypeStruct((rows, width), BF),
            jax.ShapeDtypeStruct(gates.shape[::-1], BF),
            slab,
            slab,
            jax.ShapeDtypeStruct((1, hidden // replicas, width), F32),
        ],
        in_specs=[VMEM] * 5,
        out_specs=[VMEM] * 5,
        compiler_params=pltpu.CompilerParams(vmem_limit_bytes=12 * 1024 * 1024),
    )(parts, routing.T, a, b, g_own)
    return token_grad, gate_grad.T, *sums


def solution(mesh):
    in_specs = (
        P(("dp", "expert"), None),
        P(("dp", "expert"), None),
        P(("dp", "expert"), None),
        P(("dp", "expert"), None),
        P("expert", None, None),
        P("expert", None, None),
        P("expert", None, None),
    )
    out_specs = (
        P(("dp", "expert"), None),
        P(("dp", "expert"), None),
        P("expert", "dp", None),
        P("expert", "dp", None),
        P("expert", "dp", None),
    )
    return jax.shard_map(
        on_device, mesh=mesh, in_specs=in_specs, out_specs=out_specs, check_vma=False
    )
```

```python
import functools
import math

import jax
import jax.numpy as jnp
from jax import lax
from jax.experimental import pallas as pl
from jax.experimental.pallas import tpu as pltpu
from jax.sharding import PartitionSpec as P

BF = jnp.bfloat16
F32 = jnp.float32
LANES = 128
HOP_FLOPS = 5_000_000_000
SIDE_FLOPS = 2_500_000_000
FAR_FLOPS = 15_000_000_000


def dot(a, b, ca, cb):
    return lax.dot_general(a, b, (((ca,), (cb,)), ((), ())), preferred_element_type=F32)


def pack_kernel(routing, gates, tokens, cotangent, out, named_ref, gate_ref, sems):
    rows, width = tokens.shape
    small = [pltpu.make_async_copy(routing, named_ref, sems.at[0]), pltpu.make_async_copy(gates, gate_ref, sems.at[1])]
    large = [
        pltpu.make_async_copy(tokens, out.at[:, pl.ds(0, width)], sems.at[2]),
        pltpu.make_async_copy(cotangent, out.at[:, pl.ds(width, width)], sems.at[3]),
    ]
    for copy in small + large:
        copy.start()
    for copy in small:
        copy.wait()
    expert = lax.broadcasted_iota(jnp.int32, (LANES, rows), 0)
    dense = jnp.zeros((LANES, rows), F32)
    named, gate = named_ref[...], gate_ref[...].astype(F32)
    for k in range(routing.shape[0]):
        dense = jnp.where(expert == named[k : k + 1], gate[k : k + 1], dense)
    out[:, 2 * width :] = dense.T.astype(BF)
    for copy in large:
        copy.wait()


def finish_kernel(parts, routing, p, q, r, token_grad, gate_grad, gate, up, down):
    rows, width = token_grad.shape
    total = p[...].astype(F32) + q[...].astype(F32) + r[...].astype(F32)
    token_grad[...] = total[:, :width].astype(BF)
    terms = total[:, width:].T
    expert = lax.broadcasted_iota(jnp.int32, (LANES, rows), 0)
    named = routing[...]
    picked = [
        jnp.sum(jnp.where(expert == named[k : k + 1], terms, 0.0), axis=0, keepdims=True)
        for k in range(routing.shape[0])
    ]
    gate_grad[...] = jnp.concatenate(picked, axis=0).astype(BF)
    n, hidden = gate.shape[1:]
    m = down.shape[1]
    total = jnp.sum(parts[...].astype(F32), axis=0)
    gate[0], up[0] = total[:n, :hidden], total[:n, hidden:]
    down[0] = jnp.concatenate([total[n : n + m], total[n + m :]], axis=1)


def split(blocks, width):
    x = jnp.concatenate([b[:, :width] for b in blocks], axis=0)
    dy = jnp.concatenate([b[:, width : 2 * width] for b in blocks], axis=0)
    dense = jnp.concatenate([b[:, 2 * width :] for b in blocks], axis=0).astype(F32)
    return x, dy, dense


def one_expert(x, dy, g, w_gate, w_up, w_down):
    pre_gate, pre_up = dot(x, w_gate[...], 1, 0), dot(x, w_up[...], 1, 0)
    back = dot(dy, w_down[...], 1, 1)
    sig = jax.nn.sigmoid(pre_gate)
    silu = pre_gate * sig
    act = silu * pre_up
    act_grad = g * back
    gate_pre = (act_grad * pre_up * sig * (1.0 + pre_gate * (1.0 - sig))).astype(BF)
    up_pre = (act_grad * silu).astype(BF)
    return gate_pre, up_pre, (g * act).astype(BF), jnp.sum(act * back, axis=1, keepdims=True)


def both_experts(blocks, weights, mine, out_grads):
    width = weights[0][0].shape[0]
    x, dy, dense = split(blocks, width)
    lane = lax.broadcasted_iota(jnp.int32, dense.shape, 1)
    terms = jnp.zeros(dense.shape, F32)
    grad = jnp.zeros(x.shape, F32)
    grads, acts = [], []
    for j, (w_gate, w_up, w_down) in enumerate(weights):
        here = lane == (mine if j == 0 else mine + 1 - 2 * lax.rem(mine, 2))
        g = jnp.sum(jnp.where(here, dense, 0.0), axis=1, keepdims=True)
        gate_pre, up_pre, act, term = one_expert(x, dy, g, w_gate, w_up, w_down)
        terms = terms + jnp.where(here, term, 0.0)
        grads += [gate_pre, up_pre]
        acts.append(act)
        grad = grad + dot(gate_pre, w_gate[...], 1, 1) + dot(up_pre, w_up[...], 1, 1)
    rows = blocks[0].shape[0]
    for i, out in enumerate(out_grads):
        out[:, :width] = grad[i * rows : (i + 1) * rows].astype(BF)
        out[:, width:] = terms[i * rows : (i + 1) * rows].astype(BF)
    return x, dy, grads, acts


def put(outs, where, value):
    at = 0
    for out in outs:
        wide = out.shape[-1]
        out[where] = value[..., at : at + wide]
        at += wide


def to_parts(outs, d_gu, first_row):
    nx, _, rows, _ = outs[0].shape
    n = rows * 2 // 3
    y, ys = first_row // (nx * n), d_gu.shape[0] // (nx * n)
    pieces = d_gu.astype(BF).reshape(ys, nx, n, d_gu.shape[1])
    for x in range(nx):
        put(outs, (x, slice(y, y + ys), slice(0, n)), pieces[:, x])


def down_to_parts(outs, d_down, early=()):
    nx, ny, rows, _ = outs[0].shape
    m, half = rows // 3 // 2, d_down.shape[1] // 2
    pieces = [d_down[:, c : c + half].reshape(ny, nx, m, half) for c in (0, half)]
    pieces = jnp.concatenate(pieces, axis=2)
    for x in range(nx):
        piece, where = pieces[:, x], (x, slice(0, ny), slice(rows - 2 * m, rows))
        if early:
            piece = piece + jnp.concatenate([e[where] for e in early], axis=-1).astype(F32)
        put(outs, where, piece.astype(BF))


def group_kernel(first, swap, n_blocks, expert_ref, *refs):
    blocks, refs = refs[:n_blocks], refs[n_blocks:]
    weights, refs = (refs[:3], refs[3:6]), refs[6:]
    if not first:
        (acc_gu, acc_d), refs = refs[:2], refs[2:]
    out_grads, outs = refs[:n_blocks], refs[n_blocks:]
    width, hidden = weights[0][0].shape
    x, dy, grads, acts = both_experts(blocks, weights, expert_ref[0], out_grads)
    grads = jnp.concatenate(grads, axis=1)
    for rows in steps(outs, swap, width, hidden):
        d_gu = dot(x[:, rows], grads, 0, 0)
        if not first:
            d_gu = d_gu + acc_gu[rows, :]
        if swap:
            outs[0][rows, :] = d_gu[:, : 2 * hidden]
            to_parts(outs[2:], d_gu[:, 2 * hidden :], rows.start)
        else:
            outs[0][rows, :] = d_gu
    for j, act in enumerate(acts):
        rows = slice(j * hidden, (j + 1) * hidden)
        d_down = dot(act, dy, 0, 0)
        if not first:
            d_down = d_down + acc_d[rows, :]
        if swap and j == 1:
            down_to_parts(outs[2:], d_down)
        else:
            outs[1][rows, :] = d_down


def steps(outs, swap, width, hidden):
    step = max(width // outs[2].shape[1], 2 * hidden) if swap else 2 * hidden
    return [slice(r, r + step) for r in range(0, width, step)]


def far_kernel(expert_ref, block, *refs):
    weights, (out_grad, out_pre, out_act) = (refs[:3], refs[3:6]), refs[6:]
    _, _, grads, acts = both_experts([block], weights, expert_ref[0], [out_grad])
    out_pre[...] = jnp.concatenate(grads[:2], axis=1)
    out_act[...] = acts[0]


def last_kernel(expert_ref, block, pre, act, theirs, w_gate, w_up, w_down, acc_gu, acc_d, *refs):
    *early, out, made, sems = refs
    width, hidden = w_gate.shape
    x, dy, dense = split([theirs], width)
    here = lax.broadcasted_iota(jnp.int32, dense.shape, 1) == expert_ref[0]
    g = jnp.sum(jnp.where(here, dense, 0.0), axis=1, keepdims=True)
    gate_pre, up_pre, gated, _ = one_expert(x, dy, g, w_gate, w_up, w_down)
    x = jnp.concatenate([block[:, :width], x], axis=0)
    dy = jnp.concatenate([block[:, width : 2 * width], dy], axis=0)
    grads = jnp.concatenate([pre[...], jnp.concatenate([gate_pre, up_pre], axis=1)], axis=0)
    gated = jnp.concatenate([act[...], gated], axis=0)
    nx, ny, rows, wide = out.shape
    n = rows * 2 // 3
    step = max(nx * n, hidden)
    copies = []

    def leave(*where):
        copies.append(pltpu.make_async_copy(made.at[where], out.at[where], sems.at[len(copies)]))
        copies[-1].start()

    down_to_parts([made], dot(gated, dy, 0, 0) + acc_d[...], early)
    leave(slice(None), slice(None), pl.ds(n, rows - n))
    for r in range(0, width, step):
        y, ys = r // (nx * n), step // (nx * n)
        partner = [jnp.stack([e[p, y : y + ys, :n, :] for p in range(nx)], axis=1) for e in early]
        partner = jnp.concatenate(partner, axis=-1)
        d_gu = dot(x[:, r : r + step], grads, 0, 0) + acc_gu[r : r + step, :]
        to_parts([made], d_gu + partner.reshape(step, wide).astype(F32), r)
        leave(slice(None), pl.ds(y, ys), pl.ds(0, n))
    for copy in copies:
        copy.wait()


VMEM = pl.BlockSpec(memory_space=pltpu.VMEM)


def call(kernel, out_shape, expert, operands, aliases, flops, out_specs=VMEM, scratch=()):
    return pl.pallas_call(
        kernel,
        out_shape=out_shape,
        in_specs=[pl.BlockSpec(memory_space=pltpu.SMEM)] + [VMEM] * len(operands),
        out_specs=[out_specs] * len(out_shape),
        scratch_shapes=scratch,
        input_output_aliases=aliases,
        compiler_params=pltpu.CompilerParams(vmem_limit_bytes=26 * 1024 * 1024),
        cost_estimate=pl.CostEstimate(flops=flops, bytes_accessed=16 * 1024 * 1024, transcendentals=0),
    )(expert, *operands)


def group(expert, blocks, weights, acc, replicas=()):
    rows = blocks[0].shape[0]
    width, hidden = weights[0].shape
    own = 2 * hidden if replicas else 4 * hidden
    shapes = [jax.ShapeDtypeStruct((rows, width + LANES), BF)] * len(blocks) + [
        jax.ShapeDtypeStruct((width, own), F32),
        jax.ShapeDtypeStruct((own // 2, width), F32),
    ]
    if replicas:
        shapes += [jax.ShapeDtypeStruct((*replicas, (width + 2 * hidden) // math.prod(replicas), 2 * hidden), BF)]
    n = len(blocks)
    return call(
        functools.partial(group_kernel, not acc, bool(replicas), n),
        shapes,
        expert,
        (*blocks, *weights, *acc),
        {7 + n: n, 8 + n: n + 1} if acc and not replicas else {},
        2 * n * rows * width * hidden * 16,
    )


def add_kernel(p, q, out):
    out[...] = (p[...].astype(F32) + q[...].astype(F32)).astype(BF)


def add(p, q, flops=HOP_FLOPS):
    return pl.pallas_call(
        add_kernel,
        out_shape=jax.ShapeDtypeStruct(p.shape, BF),
        in_specs=[VMEM] * 2,
        out_specs=VMEM,
        compiler_params=pltpu.CompilerParams(vmem_limit_bytes=8 * 1024 * 1024),
        cost_estimate=pl.CostEstimate(flops=flops, bytes_accessed=3 * 2 * p.size, transcendentals=0),
    )(p, q)


def after(a, *others):
    return lax.optimization_barrier((a, *others))[0]


def on_device(tokens, cotangent, routing, gates, gate_weight, up_weight, down_weight):
    groups = lax.axis_size("expert")
    replicas = lax.axis_size("dp")
    nx, ny = 1, replicas
    rows, width = tokens.shape
    hidden = gate_weight.shape[2]
    out = [(i, (i + 2 if i % 2 == 0 else i - 2) % groups) for i in range(groups)]
    home = [(b, a) for a, b in out]
    swap = [(i, i ^ 1) for i in range(groups)]
    cross = [(i, (i - 1 if i % 2 == 0 else i + 1) % groups) for i in range(groups)]
    uncross = [(b, a) for a, b in cross]

    def send(a, pairs):
        return lax.ppermute(a, "expert", pairs)

    in_hbm = pl.BlockSpec(memory_space=pltpu.HBM)
    own = pl.pallas_call(
        pack_kernel,
        out_shape=jax.ShapeDtypeStruct((rows, 2 * width + LANES), BF),
        in_specs=[in_hbm] * 4,
        out_specs=VMEM,
        scratch_shapes=[
            pltpu.VMEM(routing.shape[::-1], jnp.int32),
            pltpu.VMEM(gates.shape[::-1], BF),
            pltpu.SemaphoreType.DMA((4,)),
        ],
        compiler_params=pltpu.CompilerParams(vmem_limit_bytes=58 * 1024 * 1024),
    )(routing.T, gates.T, tokens, cotangent)
    expert = lax.axis_index("expert").astype(jnp.int32).reshape(1)

    a1 = send(own, out)
    b1 = send(own, cross)
    weights = [gate_weight[0], up_weight[0], down_weight[0]]
    weights = weights + [send(w, swap) for w in weights]
    a2 = send(a1, out)
    g_own, g_a1, *acc = group(expert, (own, a1), weights, ())
    b2 = send(b1, out)
    a3 = send(after(a2, g_a1), out)
    g_b1, g_a2, *acc = group(expert, (b1, a2), weights, acc)
    b3 = send(b2, out)
    a4 = send(after(a3, g_a2), out)
    g_b2, g_a3, *acc = group(expert, (b2, a3), weights, acc)
    g_b3, *acc, early = group(expert, (b3,), weights, acc, (nx, ny))
    early = send(early, swap)
    whole = jax.ShapeDtypeStruct(early.shape, BF)
    theirs = send(a4, swap)
    g_a4, pre, act = call(
        far_kernel,
        [
            jax.ShapeDtypeStruct((rows, width + LANES), BF),
            jax.ShapeDtypeStruct((rows, 2 * hidden), BF),
            jax.ShapeDtypeStruct((rows, hidden), BF),
        ],
        expert,
        (a4, *weights),
        {},
        FAR_FLOPS,
    )
    (parts,) = call(
        last_kernel,
        [whole],
        expert,
        (a4, pre, act, theirs, *weights[:3], *acc, early),
        {},
        2 * rows * width * hidden * 9,
        in_hbm,
        [pltpu.VMEM(whole.shape, BF), pltpu.SemaphoreType.DMA((8,))],
    )

    b = send(g_b3, home)
    a = send(g_a4, home)

    parts = lax.all_to_all(parts[0], "dp", split_axis=0, concat_axis=0, tiled=True)
    b = send(add(b, g_b2, SIDE_FLOPS), home)
    a = send(add(a, g_a3), home)
    b = send(add(b, g_b1, SIDE_FLOPS), uncross)
    a = send(add(a, g_a2), home)
    a = send(add(a, g_a1), home)
    slab = jax.ShapeDtypeStruct((1, width // replicas, hidden), F32)
    token_grad, gate_grad, *sums = pl.pallas_call(
        finish_kernel,
        out_shape=[
            jax.ShapeDtypeStruct((rows, width), BF),
            jax.ShapeDtypeStruct(gates.shape[::-1], BF),
            slab,
            slab,
            jax.ShapeDtypeStruct((1, hidden // replicas, width), F32),
        ],
        in_specs=[VMEM] * 5,
        out_specs=[VMEM] * 5,
        compiler_params=pltpu.CompilerParams(vmem_limit_bytes=12 * 1024 * 1024),
    )(parts, routing.T, a, b, g_own)
    return token_grad, gate_grad.T, *sums


def solution(mesh):
    in_specs = (
        P(("dp", "expert"), None),
        P(("dp", "expert"), None),
        P(("dp", "expert"), None),
        P(("dp", "expert"), None),
        P("expert", None, None),
        P("expert", None, None),
        P("expert", None, None),
    )
    out_specs = (
        P(("dp", "expert"), None),
        P(("dp", "expert"), None),
        P("expert", "dp", None),
        P("expert", "dp", None),
        P("expert", "dp", None),
    )
    return jax.shard_map(
        on_device, mesh=mesh, in_specs=in_specs, out_specs=out_specs, check_vma=False
    )
```
